256 devices in a mesh: tok: 16 (over x, y_hi, core), col: 8 (over z), grp: 2 (over y_lo).
Axes of the slice: x: 4, y: 4 (y_hi: 2, y_lo: 2; y = y_hi * 2 + y_lo), z: 8, core: 2. Of those that a mesh axis runs over, the one named last changes fastest.
Arguments:
- calibration: bfloat16 [24576, 4096], P(('tok', 'grp'), 'col'), may hold values from -1.1 to 1.1
- weight: float32 [4096, 4096], P(('tok', 'grp'), 'col'), may hold values from -6 to 6
- tile_mask: int32 [32, 32], P(('tok', 'grp'), 'col'), may hold values 0 or 1
- token_ids: int32 [2048], P(('tok', 'grp')), may hold values from 0 to 767
Outputs:
- new_weight: bfloat16 [4096, 4096], P(('tok', 'grp'), 'col')
- outputs: bfloat16 [2048, 4096], P('col', ('tok', 'grp'))
The draws below stay inside these ranges and needn't reach their ends.
All inputs are finite; a program needn't handle non-finite values. No bound on the sum of `tile_mask` on one device may be relied on, other than what follows from the above.
Results may differ from the reference program's by a relative error of at most 0.0019.
The reference program's roundings to bfloat16 on the way (of `chosen`) count: a program that leaves them out, or rounds other values in their place, can miss the bound.
Values may be sent and summed in bfloat16 or wider, within the bound.
No kernel may reach another device: no remote copies, remote signals or barrier semaphores. Data moves between devices by JAX's collectives and lax.ppermute only.
A program may use at most 64 MiB of HBM per device.

```python
import math
import jax
import jax.numpy as jnp
from jax import lax

D = 4096
ROWS = 4096
TILE = 128
TOK_DEV = 768
EVAL_DEV = 64
ITERS = 3
TOKENS = 24576
EVAL = 2048


def draw_calibration(key, part):
    key = jax.random.fold_in(key, 11)
    key_rough, key_cols, key_base = jax.random.split(key, 3)
    position = jnp.arange(TOKENS, dtype=jnp.float32) / TOKENS
    roughness = jax.random.uniform(key_rough, (TOKENS,), jnp.float32, -0.47, 0.47)
    row_scale = jnp.exp(math.log(10.0) * (position - 0.5) + roughness)
    col_scale = jnp.exp(jax.random.uniform(key_cols, (D,), jnp.float32, 0.0, math.log(1000.0)))
    mixture = jnp.clip(jax.random.normal(key_base, (TOKENS, D), jnp.float32), -6.0, 6.0)
    divisor = 30000.0
    return (mixture * row_scale[:, None] * col_scale[None, :] / divisor).astype(jnp.bfloat16)


def place_ends(drawn, own_key, low, top_value):
    longest = drawn.shape.index(max(drawn.shape))
    spots = []
    for shift in (0, 1):
        where = [jax.random.randint(jax.random.fold_in(own_key, axis), (), 0, length) for axis, length in enumerate(drawn.shape)]
        where[longest] = (where[longest] + shift) % drawn.shape[longest]
        spots.append(tuple(where))
    return drawn.at[spots[0]].set(low).at[spots[1]].set(top_value)


def shard_levels(own_key, extent, pieces, smallest, high):
    loudness, own = 1.0, jax.random.fold_in(own_key, 6)
    for axis_at, shards_of in pieces:
        draws = jnp.exp(jax.random.uniform(jax.random.fold_in(own, axis_at), (shards_of,), jnp.float32, smallest / len(pieces), high / len(pieces)))
        loudness = loudness * jnp.repeat(draws, extent[axis_at] // shards_of).reshape([-1 if axis == axis_at else 1 for axis in range(len(extent))])
    return loudness


def scatter_about(own_key, extent, spread, reach, pieces=(), held_as=jnp.bfloat16):
    factor_of = shard_levels(own_key, extent, pieces, -0.22, 0.18) if pieces else 1.0
    entries = jax.random.normal(own_key, extent, jnp.float32) * spread * factor_of
    return jnp.minimum(jnp.maximum(entries, -reach), reach).astype(held_as)


def setup_inputs(seed: int = 0) -> dict:
    arg_keys = jax.random.split(jax.random.key(seed), 5)
    return {
        "calibration": draw_calibration(jax.random.fold_in(arg_keys[4], 71), 0),
        "weight": scatter_about(arg_keys[1], (ROWS, D), 1.0, 6.0, ((0, 32), (1, 8)), jnp.float32),
        "tile_mask": place_ends((jax.random.randint(arg_keys[2], (ROWS // TILE, D // TILE), 0, 2) < 1).astype(jnp.int32), jax.random.fold_in(arg_keys[2], 1), 0, 1),
        "token_ids": place_ends(jax.random.randint(arg_keys[3], (EVAL,), 0, TOK_DEV), jax.random.fold_in(arg_keys[3], 1), 0, TOK_DEV - 1).astype(jnp.int32),
    }


DAMPING = 0.1


def reference(calibration, weight, tile_mask, token_ids):
    gram_matrix = jnp.dot(calibration.T, calibration, preferred_element_type=jnp.float32)
    squares = jnp.sum(jnp.square(calibration.astype(jnp.float32)))
    trace_scale = squares / D
    hessian = gram_matrix / trace_scale + DAMPING * jnp.eye(D, dtype=jnp.float32)
    keep_mask = jnp.repeat(jnp.repeat(tile_mask.astype(jnp.float32), TILE, axis=0), TILE, axis=1)
    current = weight * keep_mask
    residual = jnp.dot(current - weight, hessian, precision=lax.Precision.HIGHEST, preferred_element_type=jnp.float32)
    for iteration in range(ITERS):
        gradient = residual * keep_mask
        image_rows = jnp.dot(gradient, hessian, precision=lax.Precision.HIGHEST, preferred_element_type=jnp.float32)
        length = jnp.sum(gradient * gradient) / jnp.sum(gradient * image_rows)
        current = current - length * gradient
        residual = residual - length * image_rows
    new_weight = current.astype(jnp.bfloat16)
    blocks = jnp.arange(EVAL, dtype=jnp.int32) // EVAL_DEV
    chosen = calibration[blocks * TOK_DEV + token_ids.astype(jnp.int32)]
    outputs = jnp.dot(chosen, new_weight.T, preferred_element_type=jnp.float32).astype(jnp.bfloat16)
    return (new_weight, outputs)
```

```python
import jax
import jax.numpy as jnp
from jax import lax
from jax.sharding import Mesh, PartitionSpec as P

TILE = 128
ITERS = 3
DAMPING = 0.1

CHIPS = ("x", "yh", "yl")
PLANE = ("x", "yh", "core", "yl")
GRAM_UNIT = 8.0
TOP = 32768.0
bf16, f16, f32 = jnp.bfloat16, jnp.float16, jnp.float32


def from_col(array, offset):
    size = lax.axis_size("col")
    return lax.ppermute(array, "col", [(i, (i - offset) % size) for i in range(size)])


def swap_core(array):
    return lax.ppermute(array, "core", [(0, 1), (1, 0)])


def token_dot(left, right):
    return lax.dot_general(left, right, (((0,), (0,)), ((), ())), preferred_element_type=f32)


def split(array, parts):
    terms, rest = [], array.astype(f32)
    for _ in range(parts):
        term = lax.reduce_precision(rest, 8, 7)
        terms.append(term.astype(bf16))
        rest = rest - term
    return terms


def reduce_plane(partial, unit):
    core = lax.axis_index("core")
    half = partial.shape[0] // 2
    own = lax.dynamic_slice_in_dim(partial, core * half, half, 0)
    other = lax.dynamic_slice_in_dim(partial, (1 - core) * half, half, 0)
    chip_sum = ((own + swap_core(other)) * unit).astype(f16)
    chips = lax.axis_size(CHIPS)
    pieces = lax.all_to_all(chip_sum, CHIPS, 0, 0, tiled=True)
    pieces = pieces.reshape(chips, half // chips, partial.shape[1])
    return jnp.sum(pieces.astype(f32), axis=0).astype(f16)


def gather_plane(piece):
    chips = lax.axis_size(CHIPS)
    copies = jnp.broadcast_to(piece[None], (chips,) + piece.shape).reshape(-1, piece.shape[1])
    own = lax.all_to_all(copies, CHIPS, 0, 0, tiled=True)
    other = swap_core(own)
    first = lax.axis_index("core") == 0
    return jnp.concatenate([jnp.where(first, own, other), jnp.where(first, other, own)], axis=0)


def ring_gather(block):
    got = {0: block}
    for step in (1, 2, 3):
        got[-step] = from_col(got[1 - step], -1)
        got[step] = from_col(got[step - 1], 1)
    half = block.shape[0] // 2
    got[4] = jnp.concatenate([from_col(got[-3][:half], -1), from_col(got[3][half:], 1)], axis=0)
    return got


OFFSETS = (0, 1, -1, 2, -2, 3, -3, 4)


def per_device(calibration, weight, tile_mask, token_ids):
    width_c = calibration.shape[1]
    cols = lax.axis_size("col")
    width = width_c * cols
    rows = weight.shape[0]
    plane = lax.axis_size(PLANE)

    squares = jnp.sum(jnp.square(calibration.astype(f32)))
    chosen = jnp.take(calibration, token_ids, axis=0)
    each = chosen.shape[0] // plane
    lane = lax.broadcasted_iota(jnp.int32, (plane, 1, width_c), 2)

    def carry_row(value, count):
        hi, mid, lo = split(value, 3)
        at = lane[:count]
        row = jnp.where(at == 0, hi, jnp.where(at == 1, mid, jnp.where(at == 2, lo, jnp.zeros((), bf16))))
        return row

    def carried(row):
        return jnp.sum(row[:, 0, :3].astype(f32))

    packet = jnp.concatenate([chosen.reshape(plane, each, width_c), carry_row(squares, plane)], axis=1)
    packet = lax.all_to_all(packet, PLANE, 0, 0, tiled=True)
    plane_squares = carried(packet[:, each:])
    spread = packet[:, :each].reshape(cols, plane // cols * each, width_c)
    packet = jnp.concatenate([spread, carry_row(plane_squares, cols)], axis=1)
    packet = lax.all_to_all(packet, "col", 0, 0, tiled=True)
    trace_scale = carried(packet[:, -1:]) / width
    chosen_piece = packet[:, :-1]

    plus1, minus1 = from_col(calibration, 1), from_col(calibration, -1)
    plus2, minus2 = from_col(plus1, 1), from_col(minus1, -1)
    unit = GRAM_UNIT / trace_scale
    near = jnp.concatenate(
        [token_dot(calibration, jnp.concatenate([calibration, plus1], axis=1)), token_dot(minus1, plus1)], axis=1
    )
    near = reduce_plane(near, unit)
    far = jnp.concatenate([token_dot(minus1, plus2), token_dot(minus2, plus2)], axis=1)
    far = reduce_plane(far, unit)
    d0, d1, d2 = (near[:, i * width_c : (i + 1) * width_c] for i in range(3))
    d3, d4 = far[:, :width_c], far[:, width_c:]
    below = from_col(near[:, width_c:], -1)
    above2 = from_col(d2, 1)
    above3 = from_col(d3, 1)
    below3 = from_col(d3, -2)
    above4 = from_col(d4, 2)
    piece = jnp.concatenate([d0, d1, above2, above3, above4, below, below3], axis=1)
    gram = gather_plane(piece)
    gram_hi, gram_lo = split(gram, 2)

    expanded = jnp.broadcast_to(tile_mask.astype(f32)[:, :, None], (1, tile_mask.shape[1], TILE)).reshape(1, width_c)
    payload = jnp.concatenate([weight, jnp.broadcast_to(expanded, (8, width_c))], axis=0)
    payload, _ = lax.optimization_barrier((payload, plus2))
    payload = lax.all_gather(payload, "col", axis=0)
    place = lax.axis_index("col")
    kept, pruned = {}, {}
    for k in OFFSETS:
        block = lax.dynamic_index_in_dim(payload, lax.rem(place + k + cols, cols), 0, keepdims=False)
        mask = block[rows : rows + 1]
        kept[k] = block[:rows] * mask
        pruned[k] = block[:rows] * mask - block[:rows]

    def gram_block(part, k):
        if k >= 0:
            return part[:, k * width_c : (k + 1) * width_c], 1
        start = (4 - k) * width_c
        return part[:, start : start + width_c], 0

    def apply(blocks):
        total = jnp.zeros((rows, width_c), f32)
        for k in OFFSETS:
            hi, lo = split(blocks[k], 2)
            both = jnp.concatenate([hi, lo], axis=0)
            block, side = gram_block(gram_hi, k)
            dims = (((1,), (side,)), ((), ()))
            part = lax.dot_general(both, block, dims, preferred_element_type=f32)
            block, _ = gram_block(gram_lo, k)
            total += part[:rows] + part[rows:] + lax.dot_general(hi, block, dims, preferred_element_type=f32)
        return total * (1.0 / GRAM_UNIT) + DAMPING * blocks[0].astype(f32)

    def row_squares(blocks):
        return sum(jnp.sum(jnp.square(blocks[k].astype(f32)), axis=1, keepdims=True) for k in OFFSETS)

    bound = (width * (1.0 + DAMPING) + 1.0) / TOP

    def norm_of(blocks, scale):
        return jnp.maximum(scale * jnp.sqrt(row_squares(blocks)), 1e-30) * bound

    mask_own = expanded
    ones = jnp.ones((rows, 1), f32)
    basis = []
    blocks, scale = pruned, ones
    for _ in range(ITERS):
        image = apply(blocks) * mask_own
        new_scale = norm_of(blocks, scale)
        sent = (image * (scale / new_scale)).astype(f16)
        blocks, scale = ring_gather(sent), new_scale
        basis.append((blocks, scale))
    last = apply(blocks) * scale * mask_own

    own = [b[0].astype(f32) * s for b, s in basis] + [last]
    moments = [jnp.sum(own[(j) // 2] * own[(j + 1) // 2]) for j in range(2 * ITERS)]
    lanes = lax.broadcasted_iota(jnp.int32, (8, 128), 1)
    vector = sum(jnp.where(lanes == j, m, 0.0) for j, m in enumerate(moments))

    def all_sum(value, axes):
        count = lax.axis_size(axes)
        copies = jnp.broadcast_to(value[None], (count,) + value.shape)
        return jnp.sum(lax.all_to_all(copies, axes, 0, 0, tiled=True), axis=0)

    vector = all_sum(vector, "col")
    vector = all_sum(vector, CHIPS)
    vector = vector + swap_core(vector)
    m = [vector[0, j] for j in range(2 * ITERS)]

    poly = [jnp.ones((), f32)] + [jnp.zeros((), f32)] * (ITERS - 1)
    weights = [jnp.zeros((), f32)] * ITERS
    for step in range(ITERS):
        top = sum(poly[i] * poly[j] * m[i + j] for i in range(step + 1) for j in range(step + 1))
        low = sum(poly[i] * poly[j] * m[i + j + 1] for i in range(step + 1) for j in range(step + 1))
        length = top / low
        weights = [w + length * p for w, p in zip(weights, poly)]
        poly = [poly[i] - (length * poly[i - 1] if i else 0.0) for i in range(ITERS)]

    chosen_piece, _ = lax.optimization_barrier((chosen_piece, gram_hi))
    all_chosen = lax.all_gather(chosen_piece, PLANE, axis=0)
    all_chosen = all_chosen.reshape(plane, cols, plane // cols, each, width_c)
    all_chosen = all_chosen.transpose(1, 2, 0, 3, 4).reshape(cols, plane // cols * plane * each, width_c)

    outputs = jnp.zeros((all_chosen.shape[1], rows), f32)
    for k in OFFSETS:
        change = sum(w * s * b[k].astype(f32) for w, (b, s) in zip(weights, basis))
        rounded = (kept[k] - change).astype(bf16)
        if k == 0:
            new_weight = rounded
        picked = lax.dynamic_index_in_dim(all_chosen, lax.rem(place + k + cols, cols), 0, keepdims=False)
        outputs += lax.dot_general(picked, rounded, (((1,), (1,)), ((), ())), preferred_element_type=f32)
    return (new_weight, outputs.astype(bf16))


def solution(mesh):
    devices = mesh.devices.reshape(4, 2, 2, 8, 2)
    mesh = Mesh(devices, ("x", "yh", "core", "col", "yl"))
    placed = (P(PLANE, "col"), P(PLANE, "col"), P(PLANE, "col"), P(PLANE))
    return jax.shard_map(
        per_device,
        mesh=mesh,
        in_specs=placed,
        out_specs=(P(PLANE, "col"), P("col", PLANE)),
        check_vma=False,
    )
```

```python
import jax
import jax.numpy as jnp
from jax import lax
from jax.experimental import pallas as pl
from jax.sharding import Mesh, PartitionSpec as P

TILE = 128
ITERS = 3
DAMPING = 0.1

CHIPS = ("x", "yh", "yl")
PLANE = ("x", "yh", "core", "yl")
GRAM_UNIT = 8.0
TOP = 32768.0
bf16, f16, f32 = jnp.bfloat16, jnp.float16, jnp.float32


def from_col(array, offset):
    size = lax.axis_size("col")
    return lax.ppermute(array, "col", [(i, (i - offset) % size) for i in range(size)])


def swap_core(array):
    return lax.ppermute(array, "core", [(0, 1), (1, 0)])


def dot(left, right, side=0):
    return lax.dot_general(left, right, (((1,), (side,)), ((), ())), preferred_element_type=f32)


def together(*arrays):
    return lax.optimization_barrier(arrays)


def split(array, parts):
    terms, rest = [], array.astype(f32)
    for _ in range(parts):
        term = lax.reduce_precision(rest, 8, 7)
        terms.append(term.astype(bf16))
        rest = rest - term
    return terms


def reduce_plane(chip_sum):
    chips = lax.axis_size(CHIPS)
    rows, width = chip_sum.shape
    pieces = lax.all_to_all(chip_sum, CHIPS, 0, 0, tiled=True)
    pieces = pieces.reshape(chips, rows // chips, width)
    return jnp.sum(pieces.astype(f32), axis=0).astype(f16)


def gather_plane(piece):
    chips = lax.axis_size(CHIPS)
    copies = jnp.broadcast_to(piece[None], (chips,) + piece.shape).reshape(-1, piece.shape[1])
    return lax.all_to_all(copies, CHIPS, 0, 0, tiled=True)


def ring_gather(block):
    got = {0: block}
    for step in (1, 2, 3):
        got[-step], got[step] = together(from_col(got[1 - step], -1), from_col(got[step - 1], 1))
    half = block.shape[0] // 2
    last = jnp.concatenate([from_col(got[-3][:half], -1), from_col(got[3][half:], 1)], axis=0)
    return got, last


ORDER = (0, 1, 2, 3, 4, -1, -2, -3)


def step_weights_kernel(parts_ref, out_ref):
    parts = parts_ref[...]
    total = jnp.sum(parts.reshape(-1, 8, 128), axis=0)
    lane = lax.broadcasted_iota(jnp.int32, (8, 128), 1)
    m = [jnp.sum(jnp.where(lane == j, total, 0.0), axis=1, keepdims=True) for j in range(2 * ITERS)]
    one, zero = jnp.ones((8, 1), f32), jnp.zeros((8, 1), f32)
    poly = [one] + [zero] * (ITERS - 1)
    weights = [zero] * ITERS
    for step in range(ITERS):
        top = sum(poly[i] * poly[j] * m[i + j] for i in range(step + 1) for j in range(step + 1))
        low = sum(poly[i] * poly[j] * m[i + j + 1] for i in range(step + 1) for j in range(step + 1))
        length = top / low
        weights = [w + length * p for w, p in zip(weights, poly)]
        poly = [poly[i] - (length * poly[i - 1] if i else zero) for i in range(ITERS)]
    out_ref[...] = sum(jnp.where(lane == j, w, 0.0) for j, w in enumerate(weights))


def per_device(calibration, weight, tile_mask, token_ids):
    depth, width_c = calibration.shape
    cols = lax.axis_size("col")
    width = width_c * cols
    rows = weight.shape[0]
    plane = lax.axis_size(PLANE)
    place = lax.axis_index("col")
    core = lax.axis_index("core")
    half = width_c // 2

    plus1 = from_col(calibration, 1)
    left = calibration.T
    minus1 = from_col(left, -1)

    squares = jnp.sum(jnp.square(calibration.astype(f32)))
    picks = token_ids[:, None] == lax.broadcasted_iota(jnp.int32, (token_ids.shape[0], depth), 1)
    chosen = dot(picks.astype(bf16), calibration).astype(bf16)
    each = chosen.shape[0] // plane
    lane = lax.broadcasted_iota(jnp.int32, (plane, 1, width_c), 2)

    def carry_row(value, count):
        hi, mid, lo = split(value, 3)
        at = lane[:count]
        return jnp.where(at == 0, hi, jnp.where(at == 1, mid, jnp.where(at == 2, lo, jnp.zeros((), bf16))))

    def carried(row):
        return jnp.sum(row[:, 0, :3].astype(f32))

    packet = jnp.concatenate([chosen.reshape(plane, each, width_c), carry_row(squares, plane)], axis=1)
    packet = lax.all_to_all(packet, PLANE, 0, 0, tiled=True)

    def halves(array):
        own = lax.dynamic_slice_in_dim(array, core * half, half, 0)
        return own, lax.dynamic_slice_in_dim(array, (1 - core) * half, half, 0)

    plus1, minus1, packet = together(plus1, minus1, packet)
    plus2, minus2 = from_col(plus1, 1), from_col(minus1, -1)
    lefts = [halves(left)] * 2 + [halves(minus1)]
    rights = [calibration, plus1, plus1]
    near_other = swap_core(jnp.concatenate([dot(l[1], r) for l, r in zip(lefts, rights)], axis=1))
    near_own = [dot(l[0], r) for l, r in zip(lefts, rights)]

    plane_squares = carried(packet[:, each:])
    spread = packet[:, :each].reshape(cols, plane // cols * each, width_c)
    packet = jnp.concatenate([spread, carry_row(plane_squares, cols)], axis=1)
    packet = lax.all_to_all(packet, "col", 0, 0, tiled=True)
    trace_scale = carried(packet[:, -1:]) / width
    unit = GRAM_UNIT / trace_scale
    all_chosen = lax.all_gather(packet[:, :-1], PLANE, axis=0)

    plus2, minus2 = together(plus2, minus2)
    lefts = [halves(minus1), halves(minus2)]
    far_other = swap_core(jnp.concatenate([dot(l[1], plus2) for l in lefts], axis=1))
    far_own = [dot(l[0], plus2) for l in lefts]
    own = jnp.concatenate(near_own + far_own, axis=1)
    other = jnp.concatenate([near_other, far_other], axis=1)
    mine = reduce_plane(((own + other) * unit).astype(f16))
    c1, c2, c3, c4, c5 = (i * width_c for i in range(1, 6))
    below, above, below3, above4 = together(
        from_col(mine[:, c1:c3], -1),
        from_col(mine[:, c2:c4], 1),
        from_col(mine[:, c3:c4], -2),
        from_col(mine[:, c4:c5], 2),
    )
    half_gram = gather_plane(jnp.concatenate([mine[:, :c2], above, above4, below, below3], axis=1))
    other_gram = swap_core(half_gram)

    expanded = jnp.broadcast_to(tile_mask.astype(f32)[:, :, None], (1, tile_mask.shape[1], TILE)).reshape(1, width_c)
    payload = jnp.concatenate([weight, jnp.broadcast_to(expanded, (8, width_c))], axis=0)
    payload, _ = together(payload, plus2)
    payload = lax.all_gather(payload, "col", axis=0)

    def along(array, axis):
        return [lax.dynamic_index_in_dim(array, lax.rem(place + k + cols, cols), axis, keepdims=False) for k in ORDER]

    full = jnp.concatenate(along(payload, 0), axis=1)
    full_mask = full[rows : rows + 1]
    kept = full[:rows] * full_mask
    pruned = kept - full[:rows]
    own_pruned = weight * expanded - weight
    pruned_norm = jnp.sum(jnp.square(pruned), axis=1, keepdims=True)

    def stack(array):
        hi, lo = split(array, 2)
        return jnp.concatenate([hi, lo], axis=0)

    pruned = stack(pruned)
    pruned, pruned_norm, half_gram = together(pruned, pruned_norm, half_gram)

    first = core == 0
    gram = jnp.concatenate([jnp.where(first, half_gram, other_gram), jnp.where(first, other_gram, half_gram)], axis=0)
    gram_hi, gram_lo = split(gram, 2)
    c8 = 8 * width_c

    def down(part):
        return jnp.concatenate([part[:, i : i + width_c] for i in range(c5, c8, width_c)], axis=0)

    down_hi, down_lo = down(gram_hi), down(gram_lo)

    def product(both, hi, lo, side):
        part = dot(both, hi, side)
        return part[:rows] + part[rows:] + dot(both[:rows], lo, side)

    def finish(total, own):
        return (total * (1.0 / GRAM_UNIT) + DAMPING * own) * expanded

    bound = (width * (1.0 + DAMPING) + 1.0) / TOP

    def row_scale(square, scale):
        return jnp.maximum(scale * jnp.sqrt(square), 1e-30) * bound

    total = product(pruned[:, :c5], gram_hi[:, :c5], gram_lo[:, :c5], 1)
    total += product(pruned[:, c5:], down_hi, down_lo, 0)
    image = finish(total, own_pruned)
    scale = row_scale(pruned_norm, 1.0)
    image = image / scale

    def squares_of(array):
        return jnp.sum(jnp.square(array.astype(f32)), axis=1, keepdims=True)

    basis, owns = [], []
    for step in range(ITERS):
        sent = image.astype(f16)
        owns.append(sent.astype(f32) * scale)
        early = [jnp.sum(owns[j // 2] * owns[(j + 1) // 2]) for j in range(2 * ITERS - 1)] if step == ITERS - 1 else []
        got, last = ring_gather(sent)
        upper = jnp.concatenate([got[k] for k in (0, 1, 2, 3)], axis=1)
        lower = jnp.concatenate([got[k] for k in (-1, -2, -3)], axis=1)
        total = product(stack(upper), gram_hi[:, :c4], gram_lo[:, :c4], 1)
        total += product(stack(lower), down_hi, down_lo, 0)
        square = squares_of(upper) + squares_of(lower)
        total, square, last, *early = together(total, square, last, *early)
        total += product(stack(last), gram_hi[:, c4:c5], gram_lo[:, c4:c5], 1)
        square += squares_of(last)
        basis.append((jnp.concatenate([upper, last, lower], axis=1), scale))
        image = finish(total, sent.astype(f32))
        if step + 1 < ITERS:
            new_scale = row_scale(square, scale)
            image, scale = image * (scale / new_scale), new_scale
    moments = early + [jnp.sum(owns[-1] * (image * scale))]

    picked = jnp.concatenate(
        [
            block.reshape(plane, plane // cols, each, width_c).transpose(1, 0, 2, 3).reshape(-1, width_c)
            for block in along(all_chosen, 1)
        ],
        axis=1,
    )

    lanes = lax.broadcasted_iota(jnp.int32, (8, 128), 1)
    vector = sum(jnp.where(lanes == j, m, 0.0) for j, m in enumerate(moments))
    vector, picked = together(vector, picked)
    vector = vector + swap_core(vector)

    def exchange(value, axes):
        count = lax.axis_size(axes)
        copies = jnp.broadcast_to(value[None], (count,) + value.shape).reshape(-1, value.shape[1])
        return lax.all_to_all(copies, axes, 0, 0, tiled=True)

    vector = jnp.sum(exchange(vector, "col").reshape(cols, 8, 128), axis=0)
    coefficients = pl.pallas_call(step_weights_kernel, out_shape=jax.ShapeDtypeStruct((8, 128), f32))(
        exchange(vector, CHIPS)
    )
    change = sum(coefficients[0, j] * s * b.astype(f32) for j, (b, s) in enumerate(basis))
    rounded = (kept - change).astype(bf16)
    outputs = dot(picked, rounded, 1).astype(bf16)
    return (rounded[:, :width_c], outputs)


def solution(mesh):
    devices = mesh.devices.reshape(4, 2, 2, 8, 2)
    mesh = Mesh(devices, ("x", "yh", "core", "col", "yl"))
    placed = (P(PLANE, "col"), P(PLANE, "col"), P(PLANE, "col"), P(PLANE))
    return jax.shard_map(
        per_device,
        mesh=mesh,
        in_specs=placed,
        out_specs=(P(PLANE, "col"), P("col", PLANE)),
        check_vma=False,
    )
```

```python
import functools

import jax
import jax.numpy as jnp
from jax import lax
from jax.experimental import pallas as pl
from jax.experimental.pallas import tpu as pltpu
from jax.sharding import Mesh, PartitionSpec as P

TILE = 128
ITERS = 3
DAMPING = 0.1

CHIPS = ("x", "yh", "yl")
PLANE = ("x", "yh", "core", "yl")
GRAM_UNIT = 8.0
TOP = 32768.0
bf16, f16, f32 = jnp.bfloat16, jnp.float16, jnp.float32


def from_col(array, offset):
    size = lax.axis_size("col")
    return lax.ppermute(array, "col", [(i, (i - offset) % size) for i in range(size)])


def swap_core(array):
    return lax.ppermute(array, "core", [(0, 1), (1, 0)])


def dot(left, right, side=0):
    return lax.dot_general(left, right, (((1,), (side,)), ((), ())), preferred_element_type=f32)


def together(*arrays):
    return lax.optimization_barrier(arrays)


def split(array, parts):
    terms, rest = [], array.astype(f32)
    for _ in range(parts):
        term = lax.reduce_precision(rest, 8, 7)
        terms.append(term.astype(bf16))
        rest = rest - term
    return terms


def reduce_plane(chip_sum):
    chips = lax.axis_size(CHIPS)
    rows, width = chip_sum.shape
    pieces = lax.all_to_all(chip_sum, CHIPS, 0, 0, tiled=True)
    pieces = pieces.reshape(chips, rows // chips, width)
    return jnp.sum(pieces.astype(f32), axis=0).astype(f16)


def gather_plane(piece):
    chips = lax.axis_size(CHIPS)
    copies = jnp.broadcast_to(piece[None], (chips,) + piece.shape).reshape(-1, piece.shape[1])
    return lax.all_to_all(copies, CHIPS, 0, 0, tiled=True)


def ring_gather(block):
    got = {0: block}
    for step in (1, 2, 3):
        got[-step], got[step] = together(from_col(got[1 - step], -1), from_col(got[step - 1], 1))
    half = block.shape[0] // 2
    last = jnp.concatenate([from_col(got[-3][:half], -1), from_col(got[3][half:], 1)], axis=0)
    return got, last


ORDER = (0, 1, 2, 3, 4, -1, -2, -3)


def gram_kernel(pairs, row_ref, *refs):
    arrays, out_ref = refs[:-1], refs[-1]
    rows, width = out_ref.shape[0], arrays[-1].shape[1]
    for i, (left, right) in enumerate(pairs):
        start = pl.multiple_of(row_ref[0], rows)
        out_ref[:, i * width : (i + 1) * width] = jnp.dot(
            arrays[left][pl.ds(start, rows), :], arrays[right][...], preferred_element_type=f32
        )


def gram_part(pairs, start, arrays, rows):
    width = arrays[-1].shape[1]
    return pl.pallas_call(
        functools.partial(gram_kernel, pairs),
        in_specs=[pl.BlockSpec(memory_space=pltpu.SMEM)] + [pl.BlockSpec(memory_space=pltpu.VMEM)] * len(arrays),
        out_specs=pl.BlockSpec(memory_space=pltpu.VMEM),
        out_shape=jax.ShapeDtypeStruct((rows, width * len(pairs)), f32),
        compiler_params=pltpu.CompilerParams(vmem_limit_bytes=24 * 2**20),
        cost_estimate=pl.CostEstimate(
            flops=2 * rows * width * len(pairs) * arrays[0].shape[1], bytes_accessed=8 * 2**20, transcendentals=0
        ),
    )(start, *arrays)


def finish_kernel(spans, core_ref, parts_ref, kept_ref, *refs):
    picked_refs = refs[:2]
    refs = refs[2:]
    count = len(spans)
    stacks = [refs[j * count : (j + 1) * count] for j in range(ITERS)]
    scale_refs, (weight_ref, out_ref) = refs[ITERS * count : -2], refs[-2:]
    total = jnp.sum(parts_ref[...].reshape(-1, 8, 128), axis=0)
    m = [jnp.sum(total[j : j + 1], axis=1, keepdims=True) for j in range(2 * ITERS)]
    one, zero = jnp.ones((1, 1), f32), jnp.zeros((1, 1), f32)
    poly = [one] + [zero] * (ITERS - 1)
    weights = [zero] * ITERS
    for step in range(ITERS):
        top = sum(poly[i] * poly[j] * m[i + j] for i in range(step + 1) for j in range(step + 1))
        low = sum(poly[i] * poly[j] * m[i + j + 1] for i in range(step + 1) for j in range(step + 1))
        length = top / low
        weights = [w + length * p for w, p in zip(weights, poly)]
        poly = [poly[i] - (length * poly[i - 1] if i else zero) for i in range(ITERS)]
    factors = [w * r[...] for w, r in zip(weights, scale_refs)]
    rows, width = weight_ref.shape
    accs = [jnp.zeros((r.shape[0], rows), f32) for r in picked_refs]
    for n, (start, end) in enumerate(spans):
        for at in range(start, end, width):
            change = jnp.zeros((rows, width), f32)
            for factor, stack in zip(factors, stacks):
                block = stack[n][:, at - start : at - start + width].astype(f32)
                change = change + factor * (block[:rows] + block[rows:])
            rounded = (kept_ref[:, at : at + width] - change).astype(bf16)
            if at == 0:
                weight_ref[...] = rounded
            accs = [
                acc
                + lax.dot_general(
                    r[:, at : at + width], rounded, (((1,), (1,)), ((), ())), preferred_element_type=f32
                )
                for acc, r in zip(accs, picked_refs)
            ]
    size = out_ref.shape[0]
    e = lax.broadcasted_iota(jnp.int32, (size, size // 2), 0)
    p = lax.broadcasted_iota(jnp.int32, (size, size // 2), 1)
    block, chip_hi, core, chip_lo, inner = e >> 6, (e >> 3) & 7, (e >> 2) & 1, (e >> 1) & 1, e & 1
    found = (chip_hi * 2 + chip_lo) * 8 + block * 2 + inner
    ordered = jnp.zeros(out_ref.shape, f32)
    for n, acc in enumerate(accs):
        here = jnp.where(core == (core_ref[0] ^ n), found, -1) == p
        ordered += jnp.dot(here.astype(f32).astype(bf16), acc.astype(bf16), preferred_element_type=f32)
    out_ref[...] = ordered.astype(bf16)


def per_device(calibration, weight, tile_mask, token_ids):
    depth, width_c = calibration.shape
    cols = lax.axis_size("col")
    width = width_c * cols
    rows = weight.shape[0]
    plane = lax.axis_size(PLANE)
    place = lax.axis_index("col")
    core = lax.axis_index("core")
    half = width_c // 2

    plus1 = from_col(calibration, 1)
    left = calibration.T
    minus1 = from_col(left, -1)

    expanded = jnp.broadcast_to(tile_mask.astype(f32)[:, :, None], (1, tile_mask.shape[1], TILE)).reshape(1, width_c)
    payload = jnp.concatenate([weight, jnp.broadcast_to(expanded, (8, width_c))], axis=0)
    payload = lax.all_gather(payload, "col", axis=0)

    picks = token_ids[:, None] == lax.broadcasted_iota(jnp.int32, (token_ids.shape[0], depth), 1)
    chosen = dot(picks.astype(bf16), calibration).astype(bf16)
    each = chosen.shape[0] // plane
    squares = jnp.sum(jnp.square(calibration.astype(f32)), axis=0, keepdims=True)

    def packed(piece, sums):
        terms = jnp.concatenate(split(sums, 3), axis=0)
        terms = jnp.broadcast_to(terms[None], (piece.shape[0],) + terms.shape)
        return jnp.concatenate([piece, terms], axis=1)

    packet = lax.all_to_all(packed(chosen.reshape(plane, each, width_c), squares), PLANE, 0, 0, tiled=True)

    plus1, minus1, packet = together(plus1, minus1, packet)
    plus2, minus2 = from_col(plus1, 1), from_col(minus1, -1)
    own_at = (core * half).astype(jnp.int32).reshape(1)
    other_at = ((1 - core) * half).astype(jnp.int32).reshape(1)
    near = (left, minus1, calibration, plus1)
    near_pairs = ((0, 2), (0, 3), (1, 3))
    near_other = swap_core(gram_part(near_pairs, other_at, near, half))
    near_own = gram_part(near_pairs, own_at, near, half)

    squares = jnp.sum(packet[:, each:].astype(f32), axis=(0, 1))[None]
    spread = packet[:, :each].reshape(cols, plane // cols * each, width_c)
    packet = lax.all_to_all(packed(spread, squares), "col", 0, 0, tiled=True)
    trace_scale = jnp.sum(packet[:, plane // cols * each :].astype(f32)) / width
    unit = GRAM_UNIT / trace_scale

    plus2, minus2 = together(plus2, minus2)
    far = (minus1, minus2, plus2)
    far_pairs = ((0, 2), (1, 2))
    far_other = swap_core(gram_part(far_pairs, other_at, far, half))
    far_own = gram_part(far_pairs, own_at, far, half)
    mine = reduce_plane(
        jnp.concatenate([((near_own + near_other) * unit).astype(f16), ((far_own + far_other) * unit).astype(f16)], axis=1)
    )
    c1, c2, c3, c4, c5 = (i * width_c for i in range(1, 6))
    c8 = 8 * width_c
    below, above, below3, above4 = together(
        from_col(mine[:, c1:c3], -1),
        from_col(mine[:, c2:c4], 1),
        from_col(mine[:, c3:c4], -2),
        from_col(mine[:, c4:c5], 2),
    )
    half_gram = gather_plane(jnp.concatenate([mine[:, :c2], above, above4, below, below3], axis=1))

    def along(array, axis):
        return [lax.dynamic_index_in_dim(array, lax.rem(place + k + cols, cols), axis, keepdims=False) for k in ORDER]

    full = jnp.concatenate(along(payload, 0), axis=1)
    full_mask = full[rows : rows + 1]
    kept = full[:rows] * full_mask
    pruned = kept - full[:rows]
    own_pruned = weight * expanded - weight
    pruned_norm = jnp.sum(jnp.square(pruned), axis=1, keepdims=True)

    def stack(array):
        hi, lo = split(array, 2)
        return jnp.concatenate([hi, lo], axis=0)

    pruned = stack(pruned)
    pruned, pruned_norm, half_gram = together(pruned, pruned_norm, half_gram)

    chosen_half, _ = together(packet[:, : plane // cols * each], payload)
    chosen_half = lax.all_gather(chosen_half, CHIPS, axis=0)
    chosen_other = swap_core(chosen_half)

    gram = jnp.zeros((width_c, c8), f16)
    gram = lax.dynamic_update_slice_in_dim(gram, half_gram, core * half, 0)
    gram = lax.dynamic_update_slice_in_dim(gram, swap_core(half_gram), (1 - core) * half, 0)
    gram_hi, gram_lo = split(gram[:, :c5], 2)
    down_hi, down_lo = split(jnp.concatenate([gram[:, i : i + width_c] for i in range(c5, c8, width_c)], axis=0), 2)

    def product(both, hi, lo, side):
        part = dot(both, hi, side)
        return part[:rows] + part[rows:] + dot(both[:rows], lo, side)

    def finish(total, own):
        return (total * (1.0 / GRAM_UNIT) + DAMPING * own) * expanded

    bound = (width * (1.0 + DAMPING) + 1.0) / TOP

    def row_scale(square, scale):
        return jnp.maximum(scale * jnp.sqrt(square), 1e-30) * bound

    total = product(pruned[:, :c5], gram_hi, gram_lo, 1)
    total += product(pruned[:, c5:], down_hi, down_lo, 0)
    image = finish(total, own_pruned)
    scale = row_scale(pruned_norm, 1.0)
    image = image / scale

    def squares_of(array):
        return jnp.sum(jnp.square(array.astype(f32)), axis=1, keepdims=True)

    def moment(a, b):
        lanes = jnp.sum(a * b, axis=0, keepdims=True)
        return sum(lanes[:, i : i + 128] for i in range(0, width_c, 128))

    stacks, scales, owns = [], [], []
    for step in range(ITERS):
        sent = image.astype(f16)
        owns.append(sent.astype(f32) * scale)
        scales.append(scale)
        early = []
        if step + 1 == ITERS:
            early = [jnp.concatenate([moment(owns[j // 2], owns[(j + 1) // 2]) for j in range(2 * ITERS - 1)], axis=0)]
        got, last = ring_gather(sent)
        upper = jnp.concatenate([got[k] for k in (0, 1, 2, 3)], axis=1)
        lower = jnp.concatenate([got[k] for k in (-1, -2, -3)], axis=1)
        square = squares_of(upper) + squares_of(lower)
        upper, lower = stack(upper), stack(lower)
        total = product(upper, gram_hi[:, :c4], gram_lo[:, :c4], 1)
        total += product(lower, down_hi, down_lo, 0)
        total, square, last, *early = together(total, square, last, *early)
        square += squares_of(last)
        last = stack(last)
        total += product(last, gram_hi[:, c4:], gram_lo[:, c4:], 1)
        stacks += [upper, last, lower]
        image = finish(total, sent.astype(f32))
        if step + 1 < ITERS:
            new_scale = row_scale(square, scale)
            image, scale = image * (scale / new_scale), new_scale
    vector = jnp.concatenate(early + [moment(owns[-1], image * scale), jnp.zeros((2, 128), f32)], axis=0)

    picked = [
        jnp.concatenate([block.reshape(-1, width_c) for block in along(array, 1)], axis=1)
        for array in (chosen_half, chosen_other)
    ]
    vector, *picked = together(vector, *picked)
    vector = vector + swap_core(vector)

    def exchange(value, axes):
        count = lax.axis_size(axes)
        copies = jnp.broadcast_to(value[None], (count,) + value.shape).reshape(-1, value.shape[1])
        return lax.all_to_all(copies, axes, 0, 0, tiled=True)

    vector = jnp.sum(exchange(vector, "col").reshape(cols, 8, 128), axis=0)
    operands = [exchange(vector, CHIPS), kept, *picked, *stacks, *scales]
    return tuple(
        pl.pallas_call(
            functools.partial(finish_kernel, ((0, c4), (c4, c5), (c5, c8))),
            in_specs=[pl.BlockSpec(memory_space=pltpu.SMEM)]
            + [pl.BlockSpec(memory_space=pltpu.VMEM)] * len(operands),
            out_specs=[pl.BlockSpec(memory_space=pltpu.VMEM)] * 2,
            out_shape=[
                jax.ShapeDtypeStruct((rows, width_c), bf16),
                jax.ShapeDtypeStruct((plane * plane // cols * each, rows), bf16),
            ],
            compiler_params=pltpu.CompilerParams(vmem_limit_bytes=32 * 2**20),
        )(core.astype(jnp.int32).reshape(1), *operands)
    )


def solution(mesh):
    devices = mesh.devices.reshape(4, 2, 2, 8, 2)
    mesh = Mesh(devices, ("x", "yh", "core", "col", "yl"))
    placed = (P(PLANE, "col"), P(PLANE, "col"), P(PLANE, "col"), P(PLANE))
    return jax.shard_map(
        per_device,
        mesh=mesh,
        in_specs=placed,
        out_specs=(P(PLANE, "col"), P("col", PLANE)),
        check_vma=False,
    )
```

```python
import functools

import jax
import jax.numpy as jnp
from jax import lax
from jax.experimental import pallas as pl
from jax.experimental.pallas import tpu as pltpu
from jax.sharding import Mesh, PartitionSpec as P

TILE = 128
ITERS = 3
DAMPING = 0.1

CHIPS = ("x", "yh", "yl")
PLANE = ("x", "yh", "core", "yl")
GRAM_UNIT = 8.0
TOP = 32768.0
bf16, f16, f32 = jnp.bfloat16, jnp.float16, jnp.float32


def from_col(array, offset):
    size = lax.axis_size("col")
    return lax.ppermute(array, "col", [(i, (i - offset) % size) for i in range(size)])


def swap_core(array):
    return lax.ppermute(array, "core", [(0, 1), (1, 0)])


def dot(left, right, side=0):
    return lax.dot_general(left, right, (((1,), (side,)), ((), ())), preferred_element_type=f32)


def together(*arrays):
    return lax.optimization_barrier(arrays)


def split(array, parts):
    terms, rest = [], array.astype(f32)
    for _ in range(parts):
        term = lax.reduce_precision(rest, 8, 7)
        terms.append(term.astype(bf16))
        rest = rest - term
    return terms


def reduce_plane(chip_sum):
    chips = lax.axis_size(CHIPS)
    rows, width = chip_sum.shape
    pieces = lax.all_to_all(chip_sum, CHIPS, 0, 0, tiled=True)
    pieces = pieces.reshape(chips, rows // chips, width)
    return jnp.sum(pieces.astype(f32), axis=0).astype(f16)


def gather_plane(piece):
    chips = lax.axis_size(CHIPS)
    copies = jnp.broadcast_to(piece[None], (chips,) + piece.shape).reshape(-1, piece.shape[1])
    return lax.all_to_all(copies, CHIPS, 0, 0, tiled=True)


def ring_gather(block):
    got = {0: block}
    for step in (1, 2, 3):
        got[-step], got[step] = together(from_col(got[1 - step], -1), from_col(got[step - 1], 1))
    half = block.shape[0] // 2
    last = jnp.concatenate([from_col(got[-3][:half], -1), from_col(got[3][half:], 1)], axis=0)
    return got, last


ORDER = (0, 1, 2, 3, 4, -1, -2, -3)


def gram_kernel(pairs, row_ref, *refs):
    arrays, out_ref = refs[:-1], refs[-1]
    rows, width = out_ref.shape[0], arrays[-1].shape[1]
    for i, (left, right) in enumerate(pairs):
        start = pl.multiple_of(row_ref[0], rows)
        out_ref[:, i * width : (i + 1) * width] = jnp.dot(
            arrays[left][pl.ds(start, rows), :], arrays[right][...], preferred_element_type=f32
        )


def gram_part(pairs, start, arrays, rows):
    width = arrays[-1].shape[1]
    return pl.pallas_call(
        functools.partial(gram_kernel, pairs),
        in_specs=[pl.BlockSpec(memory_space=pltpu.SMEM)] + [pl.BlockSpec(memory_space=pltpu.VMEM)] * len(arrays),
        out_specs=pl.BlockSpec(memory_space=pltpu.VMEM),
        out_shape=jax.ShapeDtypeStruct((rows, width * len(pairs)), f32),
        compiler_params=pltpu.CompilerParams(vmem_limit_bytes=24 * 2**20),
        cost_estimate=pl.CostEstimate(
            flops=2 * rows * width * len(pairs) * arrays[0].shape[1], bytes_accessed=8 * 2**20, transcendentals=0
        ),
    )(start, *arrays)


def call(kernel, scalar, vmem, anywhere, outs, scratch, flops, limit):
    place = pl.BlockSpec(memory_space=pltpu.VMEM)
    return pl.pallas_call(
        kernel,
        in_specs=[pl.BlockSpec(memory_space=pltpu.SMEM)]
        + [place] * len(vmem)
        + [pl.BlockSpec(memory_space=pl.ANY)] * len(anywhere),
        out_specs=[place] * len(outs),
        out_shape=outs,
        scratch_shapes=scratch,
        compiler_params=pltpu.CompilerParams(vmem_limit_bytes=limit * 2**20),
        cost_estimate=pl.CostEstimate(flops=flops, bytes_accessed=10 * 2**20, transcendentals=0),
    )(scalar, *vmem, *anywhere)


def product_kernel(last, bound, core_ref, *refs):
    refs = list(refs)

    def take(count):
        taken = refs[:count]
        del refs[:count]
        return taken

    highs, lows = take(8), take(8)
    (mask_ref,), (scale_ref,) = take(1), take(1)
    earlier = take(3 * (ITERS - 1)) if last else []
    grams = take(4)
    outs = take(1 if last else 2)
    held, sems = take(4), take(1)[0]
    rows, width = highs[0].shape
    half = width // 2
    copies = []
    for n in range(8):
        group = []
        for j in range(4):
            span = pl.ds(n * width, width)
            copy = pltpu.make_async_copy(grams[j].at[:, span], held[j].at[:, span], sems.at[n, j])
            copy.start()
            group.append(copy)
        copies.append(group)
    core = core_ref[0]
    at = (pl.multiple_of(core * half, half), pl.multiple_of((1 - core) * half, half))
    sides = [jnp.zeros((rows, half), f32)] * 2
    total = jnp.zeros((rows, width), f32)
    square = jnp.zeros((rows, 1), f32)
    for n in range(8):
        high, low = highs[n][...], lows[n][...]
        value = high.astype(f32) + low.astype(f32)
        square = square + jnp.sum(value * value, axis=1, keepdims=True)
        if n == 0:
            own = value
        for copy in copies[n]:
            copy.wait()
        span = slice(n * width, (n + 1) * width)
        for side in range(2):
            gram_hi, gram_lo = held[2 * side][:, span], held[2 * side + 1][:, span]
            if n < 5:
                dims = (((1,), (1,)), ((), ()))
                x_hi, x_lo = high, low
            else:
                dims = (((1,), (0,)), ((), ()))
                x_hi, x_lo = highs[n][:, pl.ds(at[side], half)], lows[n][:, pl.ds(at[side], half)]
            both = jnp.concatenate([x_hi, x_lo], axis=0)
            part = lax.dot_general(both, gram_hi, dims, preferred_element_type=f32)
            part = part[:rows] + part[rows:]
            part += lax.dot_general(x_hi, gram_lo, dims, preferred_element_type=f32)
            if n < 5:
                sides[side] = sides[side] + part
            else:
                total = total + part
    first = core == 0
    total += jnp.concatenate(
        [jnp.where(first, sides[0], sides[1]), jnp.where(first, sides[1], sides[0])], axis=1
    )
    image = (total * (1.0 / GRAM_UNIT) + DAMPING * own) * mask_ref[...]
    scale = scale_ref[:, :1]
    if last:
        vectors = [
            (earlier[3 * j][...].astype(f32) + earlier[3 * j + 1][...].astype(f32)) * earlier[3 * j + 2][:, :1]
            for j in range(ITERS - 1)
        ] + [own * scale, image * scale]
        outs[0][...] = jnp.zeros((8, 128), f32)
        for j in range(2 * ITERS):
            lanes = jnp.sum(vectors[j // 2] * vectors[(j + 1) // 2], axis=0, keepdims=True)
            outs[0][j : j + 1, :] = sum(lanes[:, i : i + 128] for i in range(0, width, 128))
    else:
        new_scale = jnp.maximum(scale * jnp.sqrt(square), 1e-30) * bound
        outs[0][...] = image * (scale / new_scale)
        outs[1][...] = jnp.broadcast_to(new_scale, outs[1].shape)


def finish_kernel(core_ref, parts_ref, *refs):
    scale_refs, refs = refs[:ITERS], refs[ITERS:]
    count = 1 + 16 + 16 * ITERS
    sources, (weight_ref, out_ref), refs = refs[:count], refs[count : count + 2], refs[count + 2 :]
    kept_ref, picked_ref, basis_ref, kept_sems, picked_sems, basis_sems = refs
    rows, width = weight_ref.shape
    copies = []
    for n in range(8):
        span = pl.ds(n * width, width)
        group = [pltpu.make_async_copy(sources[0].at[:, span], kept_ref.at[:, span], kept_sems.at[n])]
        for j in range(2):
            i = 8 * j + n
            group.append(pltpu.make_async_copy(sources[1 + i], picked_ref.at[i], picked_sems.at[i]))
        for j in range(2 * ITERS):
            i = 8 * j + n
            group.append(pltpu.make_async_copy(sources[17 + i], basis_ref.at[i], basis_sems.at[i]))
        for copy in group:
            copy.start()
        copies.append(group)
    total = jnp.sum(parts_ref[...].reshape(-1, 8, 128), axis=0)
    m = [jnp.sum(total[j : j + 1], axis=1, keepdims=True) for j in range(2 * ITERS)]
    one, zero = jnp.ones((1, 1), f32), jnp.zeros((1, 1), f32)
    poly = [one] + [zero] * (ITERS - 1)
    weights = [zero] * ITERS
    for step in range(ITERS):
        top = sum(poly[i] * poly[j] * m[i + j] for i in range(step + 1) for j in range(step + 1))
        low = sum(poly[i] * poly[j] * m[i + j + 1] for i in range(step + 1) for j in range(step + 1))
        length = top / low
        weights = [w + length * p for w, p in zip(weights, poly)]
        poly = [poly[i] - (length * poly[i - 1] if i else zero) for i in range(ITERS)]
    factors = [w * r[:, :1] for w, r in zip(weights, scale_refs)]
    size = out_ref.shape[0]
    accs = [jnp.zeros((size // 2, rows), f32)] * 2
    for n in range(8):
        for copy in copies[n]:
            copy.wait()
        change = jnp.zeros((rows, width), f32)
        for step, factor in enumerate(factors):
            high, low = basis_ref[16 * step + n], basis_ref[16 * step + 8 + n]
            change = change + factor * (high.astype(f32) + low.astype(f32))
        rounded = (kept_ref[:, n * width : (n + 1) * width] - change).astype(bf16)
        if n == 0:
            weight_ref[...] = rounded
        accs = [acc + dot(picked_ref[8 * j + n], rounded, 1) for j, acc in enumerate(accs)]
    e = lax.broadcasted_iota(jnp.int32, (size, size // 2), 0)
    p = lax.broadcasted_iota(jnp.int32, (size, size // 2), 1)
    block, chip_hi, core, chip_lo, inner = e >> 6, (e >> 3) & 7, (e >> 2) & 1, (e >> 1) & 1, e & 1
    found = (chip_hi * 2 + chip_lo) * 8 + block * 2 + inner
    ordered = jnp.zeros(out_ref.shape, f32)
    for n, acc in enumerate(accs):
        here = jnp.where(core == (core_ref[0] ^ n), found, -1) == p
        ordered += jnp.dot(here.astype(f32).astype(bf16), acc.astype(bf16), preferred_element_type=f32)
    out_ref[...] = ordered.astype(bf16)


def per_device(calibration, weight, tile_mask, token_ids):
    depth, width_c = calibration.shape
    cols = lax.axis_size("col")
    width = width_c * cols
    rows = weight.shape[0]
    plane = lax.axis_size(PLANE)
    place = lax.axis_index("col")
    core = lax.axis_index("core")
    half = width_c // 2

    plus1 = from_col(calibration, 1)
    left = calibration.T
    minus1 = from_col(left, -1)

    picks = token_ids[:, None] == lax.broadcasted_iota(jnp.int32, (token_ids.shape[0], depth), 1)
    chosen = dot(picks.astype(bf16), calibration).astype(bf16)
    each = chosen.shape[0] // plane
    squares = jnp.sum(jnp.square(calibration.astype(f32)), axis=0, keepdims=True)

    def packed(piece, sums):
        terms = jnp.concatenate(split(sums, 3), axis=0)
        terms = jnp.broadcast_to(terms[None], (piece.shape[0],) + terms.shape)
        return jnp.concatenate([piece, terms], axis=1)

    packet = lax.all_to_all(packed(chosen.reshape(plane, each, width_c), squares), PLANE, 0, 0, tiled=True)

    plus1, minus1, packet = together(plus1, minus1, packet)
    plus2, minus2 = from_col(plus1, 1), from_col(minus1, -1)
    own_at = (core * half).astype(jnp.int32).reshape(1)
    other_at = ((1 - core) * half).astype(jnp.int32).reshape(1)
    near = (left, minus1, calibration, plus1)
    near_pairs = ((0, 2), (0, 3), (1, 3))
    near_other = swap_core(gram_part(near_pairs, other_at, near, half))
    near_own = gram_part(near_pairs, own_at, near, half)

    squares = jnp.sum(packet[:, each:].astype(f32), axis=(0, 1))[None]
    spread = packet[:, :each].reshape(cols, plane // cols * each, width_c)
    packet = lax.all_to_all(packed(spread, squares), "col", 0, 0, tiled=True)
    plus2, minus2, packet = together(plus2, minus2, packet)
    trace_scale = jnp.sum(packet[:, plane // cols * each :].astype(f32)) / width
    unit = GRAM_UNIT / trace_scale

    expanded = jnp.broadcast_to(tile_mask.astype(f32)[:, :, None], (1, tile_mask.shape[1], TILE)).reshape(1, width_c)
    payload = jnp.concatenate([weight, jnp.broadcast_to(expanded, (8, width_c))], axis=0)
    payload, _ = together(payload, plus2)
    payload = lax.all_gather(payload, "col", axis=0)

    far = (minus1, minus2, plus2)
    far_pairs = ((0, 2), (1, 2))
    far_other = swap_core(gram_part(far_pairs, other_at, far, half))
    far_own = gram_part(far_pairs, own_at, far, half)
    mine = reduce_plane(
        jnp.concatenate([((near_own + near_other) * unit).astype(f16), ((far_own + far_other) * unit).astype(f16)], axis=1)
    )
    c1, c2, c3, c4, c5 = (i * width_c for i in range(1, 6))
    c8 = 8 * width_c
    below, above, below3, above4 = together(
        from_col(mine[:, c1:c3], -1),
        from_col(mine[:, c2:c4], 1),
        from_col(mine[:, c3:c4], -2),
        from_col(mine[:, c4:c5], 2),
    )
    half_gram = gather_plane(jnp.concatenate([mine[:, :c2], above, above4, below, below3], axis=1))

    def along(array, axis):
        return [lax.dynamic_index_in_dim(array, lax.rem(place + k + cols, cols), axis, keepdims=False) for k in ORDER]

    full = jnp.concatenate(along(payload, 0), axis=1)
    full_mask = full[rows : rows + 1]
    kept = full[:rows] * full_mask
    pruned = kept - full[:rows]

    def parts(blocks):
        terms = [split(block, 2) for block in blocks]
        return [t[0] for t in terms] + [t[1] for t in terms]

    blocks = parts([pruned[:, n * width_c : (n + 1) * width_c] for n in range(8)])
    half_gram, *blocks = together(half_gram, *blocks)
    grams = split(half_gram, 2) + split(swap_core(half_gram), 2)

    chosen_half, _ = together(packet[:, : plane // cols * each], payload)
    chosen_half = lax.all_gather(chosen_half, CHIPS, axis=0)

    core_at = core.astype(jnp.int32).reshape(1)
    bound = (width * (1.0 + DAMPING) + 1.0) / TOP
    image_shape = jax.ShapeDtypeStruct((rows, width_c), f32)
    lane_shape = jax.ShapeDtypeStruct((rows, 128), f32)
    moment_shape = jax.ShapeDtypeStruct((8, 128), f32)

    def product(last, blocks, scale, earlier=()):
        return call(
            functools.partial(product_kernel, last, bound),
            core_at,
            [*blocks, expanded, scale, *earlier],
            grams,
            [moment_shape] if last else [image_shape, lane_shape],
            [pltpu.VMEM((half, c8), bf16)] * 4 + [pltpu.SemaphoreType.DMA((8, 4))],
            6 * rows * width * width_c,
            24,
        )

    image, scale = product(False, blocks, jnp.ones((rows, 128), f32))
    basis, scales, earlier = [], [], []
    for step in range(ITERS):
        (sent,) = together(image.astype(f16))
        got, last = ring_gather(sent)
        blocks = parts([last if k == 4 else got[k] for k in ORDER])
        basis += blocks
        scales.append(scale)
        if step == 0:
            chosen_half, blocks[0] = together(chosen_half, blocks[0])
            chosen_other = swap_core(chosen_half)
        if step + 1 < ITERS:
            earlier += [blocks[0], blocks[8], scale]
            image, scale = product(False, blocks, scale)
    (vector,) = product(True, blocks, scale, earlier)

    picked = [block.reshape(-1, width_c) for array in (chosen_half, chosen_other) for block in along(array, 1)]
    vector, *picked = together(vector, *picked)
    vector = vector + swap_core(vector)

    def exchange(value, axes):
        count = lax.axis_size(axes)
        copies = jnp.broadcast_to(value[None], (count,) + value.shape).reshape(-1, value.shape[1])
        return lax.all_to_all(copies, axes, 0, 0, tiled=True)

    vector = jnp.sum(exchange(vector, "col").reshape(cols, 8, 128), axis=0)
    return tuple(
        call(
            finish_kernel,
            core_at,
            [exchange(vector, CHIPS), *scales],
            [kept, *picked, *basis],
            [
                jax.ShapeDtypeStruct((rows, width_c), bf16),
                jax.ShapeDtypeStruct((plane * plane // cols * each, rows), bf16),
            ],
            [
                pltpu.VMEM((rows, width), f32),
                pltpu.VMEM((16, plane * plane // cols * each // 2, width_c), bf16),
                pltpu.VMEM((16 * ITERS, rows, width_c), bf16),
                pltpu.SemaphoreType.DMA((8,)),
                pltpu.SemaphoreType.DMA((16,)),
                pltpu.SemaphoreType.DMA((16 * ITERS,)),
            ],
            2 * 256 * rows * width,
            24,
        )
    )


def solution(mesh):
    devices = mesh.devices.reshape(4, 2, 2, 8, 2)
    mesh = Mesh(devices, ("x", "yh", "core", "col", "yl"))
    placed = (P(PLANE, "col"), P(PLANE, "col"), P(PLANE, "col"), P(PLANE))
    return jax.shard_map(
        per_device,
        mesh=mesh,
        in_specs=placed,
        out_specs=(P(PLANE, "col"), P("col", PLANE)),
        check_vma=False,
    )
```

```python
import functools

import jax
import jax.numpy as jnp
from jax import lax
from jax.experimental import pallas as pl
from jax.experimental.pallas import tpu as pltpu
from jax.sharding import Mesh, PartitionSpec as P

TILE = 128
ITERS = 3
DAMPING = 0.1

CHIPS = ("x", "yh", "yl")
PLANE = ("x", "yh", "core", "yl")
GRAM_UNIT = 8.0
TOP = 32768.0
bf16, f16, f32 = jnp.bfloat16, jnp.float16, jnp.float32


def from_col(array, offset):
    size = lax.axis_size("col")
    return lax.ppermute(array, "col", [(i, (i - offset) % size) for i in range(size)])


def swap_core(array):
    return lax.ppermute(array, "core", [(0, 1), (1, 0)])


def dot(left, right, side=0):
    return lax.dot_general(left, right, (((1,), (side,)), ((), ())), preferred_element_type=f32)


def together(*arrays):
    return lax.optimization_barrier(arrays)


def split(array, parts):
    terms, rest = [], array.astype(f32)
    for _ in range(parts):
        term = lax.reduce_precision(rest, 8, 7)
        terms.append(term.astype(bf16))
        rest = rest - term
    return terms


def reduce_plane(chip_sum):
    chips = lax.axis_size(CHIPS)
    rows, width = chip_sum.shape
    pieces = lax.all_to_all(chip_sum, CHIPS, 0, 0, tiled=True)
    pieces = pieces.reshape(chips, rows // chips, width)
    return jnp.sum(pieces.astype(f32), axis=0).astype(f16)


def gather_plane(piece):
    chips = lax.axis_size(CHIPS)
    copies = jnp.broadcast_to(piece[None], (chips,) + piece.shape).reshape(-1, piece.shape[1])
    return lax.all_to_all(copies, CHIPS, 0, 0, tiled=True)


def ring_gather(block):
    got = {0: block}
    for step in (1, 2, 3):
        got[-step], got[step] = together(from_col(got[1 - step], -1), from_col(got[step - 1], 1))
    half = block.shape[0] // 2
    last = jnp.concatenate([from_col(got[-3][:half], -1), from_col(got[3][half:], 1)], axis=0)
    return got, last


ORDER = (0, 1, 2, 3, 4, -1, -2, -3)


def gram_kernel(pairs, row_ref, *refs):
    arrays, out_ref = refs[:-1], refs[-1]
    rows, width = out_ref.shape[0], arrays[-1].shape[1]
    for i, (left, right) in enumerate(pairs):
        start = pl.multiple_of(row_ref[0], rows)
        out_ref[:, i * width : (i + 1) * width] = jnp.dot(
            arrays[left][pl.ds(start, rows), :], arrays[right][...], preferred_element_type=f32
        )


def gram_part(pairs, start, arrays, rows):
    width = arrays[-1].shape[1]
    return pl.pallas_call(
        functools.partial(gram_kernel, pairs),
        in_specs=[pl.BlockSpec(memory_space=pltpu.SMEM)] + [pl.BlockSpec(memory_space=pltpu.VMEM)] * len(arrays),
        out_specs=pl.BlockSpec(memory_space=pltpu.VMEM),
        out_shape=jax.ShapeDtypeStruct((rows, width * len(pairs)), f32),
        compiler_params=pltpu.CompilerParams(vmem_limit_bytes=8 * 2**20),
        cost_estimate=pl.CostEstimate(
            flops=2 * rows * width * len(pairs) * arrays[0].shape[1], bytes_accessed=8 * 2**20, transcendentals=0
        ),
    )(start, *arrays)


def product_kernel(first, last, bound, core_ref, *refs):
    refs = list(refs)

    def take(count):
        taken = refs[:count]
        del refs[:count]
        return taken

    highs, lows = take(8), take(8)
    (mask_ref,), (scale_ref,) = take(1), take(1)
    earlier = take(ITERS - 1) if last else []
    grams = take(4)
    outs = take(1 if last else 2)
    scaled_ref = None if first else take(1)[0]
    held, sems = take(4), take(1)[0]
    rows, width = highs[0].shape
    half = width // 2
    copies = []
    for n in range(8):
        group = []
        for j in range(4):
            span = pl.ds(n * width, width)
            copy = pltpu.make_async_copy(grams[j].at[:, span], held[j].at[:, span], sems.at[n, j])
            copy.start()
            group.append(copy)
        copies.append(group)
    core = core_ref[0]
    at = (pl.multiple_of(core * half, half), pl.multiple_of((1 - core) * half, half))
    sides = [jnp.zeros((rows, half), f32)] * 2
    total = jnp.zeros((rows, width), f32)
    square = jnp.zeros((rows, 1), f32)
    for n in range(8):
        high, low = highs[n][...], lows[n][...]
        value = high.astype(f32) + low.astype(f32)
        square = square + jnp.sum(value * value, axis=1, keepdims=True)
        if n == 0:
            own = value
        if not first:
            scaled_ref[:, n * width : (n + 1) * width] = value * scale_ref[:, :1]
        for copy in copies[n]:
            copy.wait()
        span = slice(n * width, (n + 1) * width)
        for side in range(2):
            gram_hi, gram_lo = held[2 * side][:, span], held[2 * side + 1][:, span]
            if n < 5:
                dims = (((1,), (1,)), ((), ()))
                x_hi, x_lo = high, low
            else:
                dims = (((1,), (0,)), ((), ()))
                x_hi, x_lo = highs[n][:, pl.ds(at[side], half)], lows[n][:, pl.ds(at[side], half)]
            both = jnp.concatenate([x_hi, x_lo], axis=0)
            part = lax.dot_general(both, gram_hi, dims, preferred_element_type=f32)
            part = part[:rows] + part[rows:]
            part += lax.dot_general(x_hi, gram_lo, dims, preferred_element_type=f32)
            if n < 5:
                sides[side] = sides[side] + part
            else:
                total = total + part
    lower = core == 0
    total += jnp.concatenate(
        [jnp.where(lower, sides[0], sides[1]), jnp.where(lower, sides[1], sides[0])], axis=1
    )
    image = (total * (1.0 / GRAM_UNIT) + DAMPING * own) * mask_ref[...]
    scale = scale_ref[:, :1]
    if last:
        vectors = [r[...] for r in earlier] + [own * scale, image * scale]
        outs[0][...] = jnp.zeros((8, 128), f32)
        for j in range(2 * ITERS):
            lanes = jnp.sum(vectors[j // 2] * vectors[(j + 1) // 2], axis=0, keepdims=True)
            outs[0][j : j + 1, :] = sum(lanes[:, i : i + 128] for i in range(0, width, 128))
    else:
        new_scale = jnp.maximum(scale * jnp.sqrt(square), 1e-30) * bound
        outs[0][...] = image * (scale / new_scale)
        outs[1][...] = jnp.broadcast_to(new_scale, outs[1].shape)


def finish_kernel(info_ref, parts_ref, payload_ref, *refs):
    basis_refs, picked_refs = refs[:ITERS], refs[ITERS : ITERS + 2]
    weight_ref, out_ref, lengths_ref, acc_ref = refs[ITERS + 2 :]
    n = pl.program_id(0)
    rows = weight_ref.shape[0]
    size = out_ref.shape[0]

    @pl.when(n == 0)
    def _():
        total = jnp.sum(parts_ref[...].reshape(-1, 8, 128), axis=0)
        m = [jnp.sum(total[j : j + 1], axis=1, keepdims=True) for j in range(2 * ITERS)]
        one, zero = jnp.ones((1, 1), f32), jnp.zeros((1, 1), f32)
        poly = [one] + [zero] * (ITERS - 1)
        weights = [zero] * ITERS
        for step in range(ITERS):
            top = sum(poly[i] * poly[j] * m[i + j] for i in range(step + 1) for j in range(step + 1))
            low = sum(poly[i] * poly[j] * m[i + j + 1] for i in range(step + 1) for j in range(step + 1))
            length = top / low
            weights = [w + length * p for w, p in zip(weights, poly)]
            poly = [poly[i] - (length * poly[i - 1] if i else zero) for i in range(ITERS)]
        for j in range(ITERS):
            lengths_ref[j : j + 1, :] = jnp.broadcast_to(weights[j], (1, 128))
        acc_ref[...] = jnp.zeros_like(acc_ref)

    change = sum(lengths_ref[j : j + 1, :1] * basis_refs[j][...] for j in range(ITERS))
    rounded = (payload_ref[0, :rows, :] * payload_ref[0, rows : rows + 1, :] - change).astype(bf16)

    @pl.when(n == 0)
    def _():
        weight_ref[...] = rounded

    for j, picked_ref in enumerate(picked_refs):
        acc_ref[j * size // 2 : (j + 1) * size // 2, :] += dot(picked_ref[0], rounded, 1)

    @pl.when(n == pl.num_programs(0) - 1)
    def _():
        e = lax.broadcasted_iota(jnp.int32, (size, size), 0)
        p = lax.broadcasted_iota(jnp.int32, (size, size), 1)
        block, chip_hi, core, chip_lo, inner = e >> 6, (e >> 3) & 7, (e >> 2) & 1, (e >> 1) & 1, e & 1
        found = (core ^ info_ref[8]) * (size // 2) + (chip_hi * 2 + chip_lo) * 8 + block * 2 + inner
        here = (found == p).astype(f32).astype(bf16)
        out_ref[...] = dot(here, acc_ref[...].astype(bf16)).astype(bf16)


def per_device(calibration, weight, tile_mask, token_ids):
    depth, width_c = calibration.shape
    cols = lax.axis_size("col")
    width = width_c * cols
    rows = weight.shape[0]
    plane = lax.axis_size(PLANE)
    place = lax.axis_index("col")
    core = lax.axis_index("core")
    half = width_c // 2

    plus1 = from_col(calibration, 1)
    left = calibration.T
    minus1 = from_col(left, -1)

    picks = token_ids[:, None] == lax.broadcasted_iota(jnp.int32, (token_ids.shape[0], depth), 1)
    chosen = dot(picks.astype(bf16), calibration).astype(bf16)
    each = chosen.shape[0] // plane
    squares = jnp.sum(jnp.square(calibration.astype(f32)), axis=0, keepdims=True)

    def packed(piece, sums):
        terms = jnp.concatenate(split(sums, 3), axis=0)
        terms = jnp.broadcast_to(terms[None], (piece.shape[0],) + terms.shape)
        return jnp.concatenate([piece, terms], axis=1)

    packet = lax.all_to_all(packed(chosen.reshape(plane, each, width_c), squares), PLANE, 0, 0, tiled=True)

    plus1, minus1, packet = together(plus1, minus1, packet)
    plus2, minus2 = from_col(plus1, 1), from_col(minus1, -1)
    own_at = (core * half).astype(jnp.int32).reshape(1)
    other_at = ((1 - core) * half).astype(jnp.int32).reshape(1)
    near = (left, minus1, calibration, plus1)
    near_pairs = ((0, 2), (0, 3), (1, 3))
    near_other = swap_core(gram_part(near_pairs, other_at, near, half))
    near_own = gram_part(near_pairs, own_at, near, half)

    squares = jnp.sum(packet[:, each:].astype(f32), axis=(0, 1))[None]
    spread = packet[:, :each].reshape(cols, plane // cols * each, width_c)
    packet = lax.all_to_all(packed(spread, squares), "col", 0, 0, tiled=True)
    plus2, minus2, packet = together(plus2, minus2, packet)
    trace_scale = jnp.sum(packet[:, plane // cols * each :].astype(f32)) / width
    unit = GRAM_UNIT / trace_scale

    expanded = jnp.broadcast_to(tile_mask.astype(f32)[:, :, None], (1, tile_mask.shape[1], TILE)).reshape(1, width_c)
    payload = jnp.concatenate([weight, jnp.broadcast_to(expanded, (8, width_c))], axis=0)
    payload, _ = together(payload, plus2)
    payload = lax.all_gather(payload, "col", axis=0)

    far = (minus1, minus2, plus2)
    far_pairs = ((0, 2), (1, 2))
    far_other = swap_core(gram_part(far_pairs, other_at, far, half))
    far_own = gram_part(far_pairs, own_at, far, half)
    mine = reduce_plane(
        jnp.concatenate([((near_own + near_other) * unit).astype(f16), ((far_own + far_other) * unit).astype(f16)], axis=1)
    )
    c1, c2, c3, c4, c5 = (i * width_c for i in range(1, 6))
    c8 = 8 * width_c
    below, above, below3, above4 = together(
        from_col(mine[:, c1:c3], -1),
        from_col(mine[:, c2:c4], 1),
        from_col(mine[:, c3:c4], -2),
        from_col(mine[:, c4:c5], 2),
    )
    half_gram = gather_plane(jnp.concatenate([mine[:, :c2], above, above4, below, below3], axis=1))

    def along(array, axis):
        return [lax.dynamic_index_in_dim(array, lax.rem(place + k + cols, cols), axis, keepdims=False) for k in ORDER]

    def parts(blocks):
        terms = [split(block, 2) for block in blocks]
        return [t[0] for t in terms] + [t[1] for t in terms]

    blocks = parts([b[:rows] * (b[rows : rows + 1] - 1.0) for b in along(payload, 0)])
    half_gram, *blocks = together(half_gram, *blocks)
    grams = split(half_gram, 2) + split(swap_core(half_gram), 2)

    chosen_half, _ = together(packet[:, : plane // cols * each], payload)
    chosen_half = lax.all_gather(chosen_half, CHIPS, axis=0)

    core_at = core.astype(jnp.int32).reshape(1)
    bound = (width * (1.0 + DAMPING) + 1.0) / TOP
    image_shape = jax.ShapeDtypeStruct((rows, width_c), f32)
    lane_shape = jax.ShapeDtypeStruct((rows, 128), f32)
    moment_shape = jax.ShapeDtypeStruct((8, 128), f32)
    whole_shape = jax.ShapeDtypeStruct((rows, width), f32)

    def product(first, last, blocks, scale, earlier=()):
        whole = pl.BlockSpec(memory_space=pltpu.VMEM)
        outs = ([moment_shape] if last else [image_shape, lane_shape]) + ([] if first else [whole_shape])
        return pl.pallas_call(
            functools.partial(product_kernel, first, last, bound),
            in_specs=[pl.BlockSpec(memory_space=pltpu.SMEM)]
            + [whole] * (len(blocks) + 2 + len(earlier))
            + [pl.BlockSpec(memory_space=pl.ANY)] * 4,
            out_specs=[whole] * len(outs),
            out_shape=outs,
            scratch_shapes=[pltpu.VMEM((half, c8), bf16)] * 4 + [pltpu.SemaphoreType.DMA((8, 4))],
            compiler_params=pltpu.CompilerParams(vmem_limit_bytes=20 * 2**20),
            cost_estimate=pl.CostEstimate(
                flops=6 * rows * width * width_c, bytes_accessed=10 * 2**20, transcendentals=0
            ),
        )(core_at, *blocks, expanded, scale, *earlier, *grams)

    image, scale = product(True, False, blocks, jnp.ones((rows, 128), f32))
    basis = []
    for step in range(ITERS):
        (sent,) = together(image.astype(f16))
        got, last = ring_gather(sent)
        blocks = parts([last if k == 4 else got[k] for k in ORDER])
        if step + 2 == ITERS:
            chosen_half, blocks[0] = together(chosen_half, blocks[0])
            chosen_other = swap_core(chosen_half)
        if step + 1 < ITERS:
            image, scale, scaled = product(False, False, blocks, scale)
        else:
            vector, scaled = product(False, True, blocks, scale, [b[:, :width_c] for b in basis])
        basis.append(scaled)

    picked = [array.transpose(1, 0, 2, 3).reshape(cols, -1, width_c) for array in (chosen_half, chosen_other)]
    vector, *picked = together(vector, *picked)
    vector = vector + swap_core(vector)

    def exchange(value, axes):
        count = lax.axis_size(axes)
        copies = jnp.broadcast_to(value[None], (count,) + value.shape).reshape(-1, value.shape[1])
        return lax.all_to_all(copies, axes, 0, 0, tiled=True)

    vector = jnp.sum(exchange(vector, "col").reshape(cols, 8, 128), axis=0)
    info = jnp.stack([lax.rem(place + k + cols, cols) for k in ORDER] + [core]).astype(jnp.int32)
    size = 2 * picked[0].shape[1]
    flat = lambda n, info: (0, 0)
    placed = lambda n, info: (info[n], 0, 0)
    return tuple(
        pl.pallas_call(
            finish_kernel,
            grid_spec=pltpu.PrefetchScalarGridSpec(
                num_scalar_prefetch=1,
                grid=(8,),
                in_specs=[pl.BlockSpec((128, 128), flat), pl.BlockSpec((1, rows + 8, width_c), placed)]
                + [pl.BlockSpec((rows, width_c), lambda n, info: (0, n))] * ITERS
                + [pl.BlockSpec((1, size // 2, width_c), placed)] * 2,
                out_specs=[pl.BlockSpec((rows, width_c), flat), pl.BlockSpec((size, rows), flat)],
                scratch_shapes=[pltpu.VMEM((8, 128), f32), pltpu.VMEM((size, rows), f32)],
            ),
            out_shape=[jax.ShapeDtypeStruct((rows, width_c), bf16), jax.ShapeDtypeStruct((size, rows), bf16)],
            compiler_params=pltpu.CompilerParams(vmem_limit_bytes=12 * 2**20),
        )(info, exchange(vector, CHIPS), *(pltpu.with_memory_space_constraint(a, pltpu.HBM) for a in (payload, *basis, *picked)))
    )


def solution(mesh):
    devices = mesh.devices.reshape(4, 2, 2, 8, 2)
    mesh = Mesh(devices, ("x", "yh", "core", "col", "yl"))
    placed = (P(PLANE, "col"), P(PLANE, "col"), P(PLANE, "col"), P(PLANE))
    return jax.shard_map(
        per_device,
        mesh=mesh,
        in_specs=placed,
        out_specs=(P(PLANE, "col"), P("col", PLANE)),
        check_vma=False,
    )
```

```python
import functools

import jax
import jax.numpy as jnp
from jax import lax
from jax.experimental import pallas as pl
from jax.experimental.pallas import tpu as pltpu
from jax.sharding import Mesh, PartitionSpec as P

TILE = 128
ITERS = 3
SUB = 2
DAMPING = 0.1

CHIPS = ("x", "yh", "yl")
PLANE = ("x", "yh", "core", "yl")
GRAM_UNIT = 8.0
TOP = 32768.0
bf16, f16, f32 = jnp.bfloat16, jnp.float16, jnp.float32


def from_col(array, offset):
    size = lax.axis_size("col")
    return lax.ppermute(array, "col", [(i, (i - offset) % size) for i in range(size)])


def swap_core(array):
    return lax.ppermute(array, "core", [(0, 1), (1, 0)])


def dot(left, right, side=0):
    return lax.dot_general(left, right, (((1,), (side,)), ((), ())), preferred_element_type=f32)


def together(*arrays):
    return lax.optimization_barrier(arrays)


def split(array, parts):
    terms, rest = [], array.astype(f32)
    for _ in range(parts):
        term = lax.reduce_precision(rest, 8, 7)
        terms.append(term.astype(bf16))
        rest = rest - term
    return terms


def reduce_plane(chip_sum):
    chips = lax.axis_size(CHIPS)
    rows, width = chip_sum.shape
    pieces = lax.all_to_all(chip_sum, CHIPS, 0, 0, tiled=True)
    pieces = pieces.reshape(chips, rows // chips, width)
    return jnp.sum(pieces.astype(f32), axis=0).astype(f16)


def gather_plane(piece):
    chips = lax.axis_size(CHIPS)
    copies = jnp.broadcast_to(piece[None], (chips,) + piece.shape).reshape(-1, piece.shape[1])
    return lax.all_to_all(copies, CHIPS, 0, 0, tiled=True)


def ring_gather(block):
    got = {0: block}
    for step in (1, 2, 3):
        got[-step], got[step] = from_col(got[1 - step], -1), from_col(got[step - 1], 1)
    half = block.shape[0] // 2
    last = jnp.concatenate([from_col(got[-3][:half], -1), from_col(got[3][half:], 1)], axis=0)
    return got, last


ORDER = (0, 1, 2, 3, 4, -1, -2, -3)


def gram_kernel(pairs, row_ref, *refs):
    arrays, out_ref = refs[:-1], refs[-1]
    rows, width = out_ref.shape[0], arrays[-1].shape[1]
    for i, (left, right) in enumerate(pairs):
        start = pl.multiple_of(row_ref[0], rows)
        out_ref[:, i * width : (i + 1) * width] = jnp.dot(
            arrays[left][pl.ds(start, rows), :], arrays[right][...], preferred_element_type=f32
        )


def gram_part(pairs, start, arrays, rows):
    width = arrays[-1].shape[1]
    return pl.pallas_call(
        functools.partial(gram_kernel, pairs),
        in_specs=[pl.BlockSpec(memory_space=pltpu.SMEM)] + [pl.BlockSpec(memory_space=pltpu.VMEM)] * len(arrays),
        out_specs=pl.BlockSpec(memory_space=pltpu.VMEM),
        out_shape=jax.ShapeDtypeStruct((rows, width * len(pairs)), f32),
        compiler_params=pltpu.CompilerParams(vmem_limit_bytes=12 * 2**20),
        cost_estimate=pl.CostEstimate(
            flops=2 * rows * width * len(pairs) * arrays[0].shape[1], bytes_accessed=8 * 2**20, transcendentals=0
        ),
    )(start, *arrays)


def product_kernel(first, last, bound, core_ref, *refs):
    refs = list(refs)

    def take(count):
        taken = refs[:count]
        del refs[:count]
        return taken

    highs, lows = take(8), take(8)
    (mask_ref,), (scale_ref,) = take(1), take(1)
    earlier = take(ITERS - 1) if last else []
    grams = take(4)
    outs = take(1 if last else 2)
    scaled_ref = None if first else take(1)[0]
    held, sems = take(4), take(1)[0]
    rows, width = highs[0].shape
    half = width // 2
    copies = []
    for n in range(8):
        group = []
        for j in range(4):
            span = pl.ds(n * width, width)
            copy = pltpu.make_async_copy(grams[j].at[:, span], held[j].at[:, span], sems.at[n, j])
            copy.start()
            group.append(copy)
        copies.append(group)
    core = core_ref[0]
    at = (pl.multiple_of(core * half, half), pl.multiple_of((1 - core) * half, half))
    sides = [jnp.zeros((rows, half), f32)] * 2
    total = jnp.zeros((rows, width), f32)
    square = jnp.zeros((rows, 1), f32)
    for n in range(8):
        high, low = highs[n][...], lows[n][...]
        value = high.astype(f32) + low.astype(f32)
        square = square + jnp.sum(value * value, axis=1, keepdims=True)
        if n == 0:
            own = value
        if not first:
            scaled_ref[:, n * width : (n + 1) * width] = value * scale_ref[:, :1]
        for copy in copies[n]:
            copy.wait()
        span = slice(n * width, (n + 1) * width)
        for side in range(2):
            gram_hi, gram_lo = held[2 * side][:, span], held[2 * side + 1][:, span]
            if n < 5:
                dims = (((1,), (1,)), ((), ()))
                x_hi, x_lo = high, low
            else:
                dims = (((1,), (0,)), ((), ()))
                x_hi, x_lo = highs[n][:, pl.ds(at[side], half)], lows[n][:, pl.ds(at[side], half)]
            both = jnp.concatenate([x_hi, x_lo], axis=0)
            part = lax.dot_general(both, gram_hi, dims, preferred_element_type=f32)
            part = part[:rows] + part[rows:]
            part += lax.dot_general(x_hi, gram_lo, dims, preferred_element_type=f32)
            if n < 5:
                sides[side] = sides[side] + part
            else:
                total = total + part
    lower = core == 0
    total += jnp.concatenate(
        [jnp.where(lower, sides[0], sides[1]), jnp.where(lower, sides[1], sides[0])], axis=1
    )
    image = (total * (1.0 / GRAM_UNIT) + DAMPING * own) * mask_ref[...]
    scale = scale_ref[:, :1]
    if last:
        vectors = [r[...] for r in earlier] + [own * scale, image * scale]
        outs[0][...] = jnp.zeros((8, 128), f32)
        for j in range(2 * ITERS):
            lanes = jnp.sum(vectors[j // 2] * vectors[(j + 1) // 2], axis=0, keepdims=True)
            outs[0][j : j + 1, :] = sum(lanes[:, i : i + 128] for i in range(0, width, 128))
    else:
        new_scale = jnp.maximum(scale * jnp.sqrt(square), 1e-30) * bound
        outs[0][...] = image * (scale / new_scale)
        outs[1][...] = jnp.broadcast_to(new_scale, outs[1].shape)


def finish_kernel(info_ref, parts_ref, *refs):
    payload_refs, basis_refs = refs[:SUB], refs[SUB : SUB + ITERS]
    picked_refs = refs[SUB + ITERS : 3 * SUB + ITERS]
    weight_ref, out_ref, lengths_ref, acc_ref = refs[3 * SUB + ITERS :]
    n = pl.program_id(0)
    rows = weight_ref.shape[0]
    size = out_ref.shape[0]

    @pl.when(n == 0)
    def _():
        total = jnp.sum(parts_ref[...].reshape(-1, 8, 128), axis=0)
        m = [jnp.sum(total[j : j + 1], axis=1, keepdims=True) for j in range(2 * ITERS)]
        one, zero = jnp.ones((1, 1), f32), jnp.zeros((1, 1), f32)
        poly = [one] + [zero] * (ITERS - 1)
        weights = [zero] * ITERS
        for step in range(ITERS):
            top = sum(poly[i] * poly[j] * m[i + j] for i in range(step + 1) for j in range(step + 1))
            low = sum(poly[i] * poly[j] * m[i + j + 1] for i in range(step + 1) for j in range(step + 1))
            length = top / low
            weights = [w + length * p for w, p in zip(weights, poly)]
            poly = [poly[i] - (length * poly[i - 1] if i else zero) for i in range(ITERS)]
        for j in range(ITERS):
            lengths_ref[j : j + 1, :] = jnp.broadcast_to(weights[j], (1, 128))
        acc_ref[...] = jnp.zeros_like(acc_ref)

    width = weight_ref.shape[1]
    for u, payload_ref in enumerate(payload_refs):
        span = slice(u * width, (u + 1) * width)
        change = sum(lengths_ref[j : j + 1, :1] * basis_refs[j][:, span] for j in range(ITERS))
        rounded = (payload_ref[0, :rows, :] * payload_ref[0, rows : rows + 1, :] - change).astype(bf16)
        if u == 0:

            @pl.when(n == 0)
            def _():
                weight_ref[...] = rounded

        for j, picked_ref in enumerate(picked_refs[2 * u : 2 * u + 2]):
            acc_ref[j * size // 2 : (j + 1) * size // 2, :] += dot(
                picked_ref[...].reshape(size // 2, width), rounded, 1
            )

    @pl.when(n == pl.num_programs(0) - 1)
    def _():
        e = lax.broadcasted_iota(jnp.int32, (size, size), 0)
        p = lax.broadcasted_iota(jnp.int32, (size, size), 1)
        block, chip_hi, core, chip_lo, inner = e >> 6, (e >> 3) & 7, (e >> 2) & 1, (e >> 1) & 1, e & 1
        found = (core ^ info_ref[8]) * (size // 2) + (chip_hi * 2 + chip_lo) * 8 + block * 2 + inner
        here = (found == p).astype(f32).astype(bf16)
        out_ref[...] = dot(here, acc_ref[...].astype(bf16)).astype(bf16)


def per_device(calibration, weight, tile_mask, token_ids):
    depth, width_c = calibration.shape
    cols = lax.axis_size("col")
    width = width_c * cols
    rows = weight.shape[0]
    plane = lax.axis_size(PLANE)
    place = lax.axis_index("col")
    core = lax.axis_index("core")
    half = width_c // 2

    plus1 = from_col(calibration, 1)
    left = calibration.T
    minus1 = from_col(left, -1)

    picks = token_ids[:, None] == lax.broadcasted_iota(jnp.int32, (token_ids.shape[0], depth), 1)
    chosen = dot(picks.astype(bf16), calibration).astype(bf16)
    each = chosen.shape[0] // plane
    squares = jnp.sum(jnp.square(calibration.astype(f32)), axis=0, keepdims=True)

    def exchange(value, axes):
        count = lax.axis_size(axes)
        copies = jnp.broadcast_to(value[None], (count,) + value.shape).reshape(-1, value.shape[1])
        return lax.all_to_all(copies, axes, 0, 0, tiled=True)

    squares = sum(squares[:, i : i + 128] for i in range(0, width_c, 128))
    squares = exchange(jnp.pad(squares, ((0, 7), (0, 0))), "col")
    plus1, minus1, squares = together(plus1, minus1, squares)
    squares = jnp.pad(jnp.sum(squares, axis=0, keepdims=True), ((0, 0), (0, width_c - 128)))
    terms = jnp.concatenate(split(squares, 3), axis=0)
    terms = jnp.broadcast_to(terms[None], (plane,) + terms.shape)
    packet = jnp.concatenate([chosen.reshape(plane, each, width_c), terms], axis=1)
    packet = lax.all_to_all(packet, PLANE, 0, 0, tiled=True)

    plus2, minus2 = from_col(plus1, 1), from_col(minus1, -1)
    own_at = (core * half).astype(jnp.int32).reshape(1)
    other_at = ((1 - core) * half).astype(jnp.int32).reshape(1)
    plus2, minus2, packet = together(plus2, minus2, packet)
    unit = GRAM_UNIT * width / jnp.sum(packet[:, each:].astype(f32))
    spread = packet[:, :each].reshape(cols, plane // cols * each, width_c)

    expanded = jnp.broadcast_to(tile_mask.astype(f32)[:, :, None], (1, tile_mask.shape[1], TILE)).reshape(1, width_c)
    payload = jnp.concatenate([weight, jnp.broadcast_to(expanded, (8, width_c))], axis=0)
    payload, _ = together(payload, plus2)
    payload = lax.all_gather(payload, "col", axis=0)

    arrays = (left, minus1, minus2, calibration, plus1, plus2)
    pairs = ((0, 3), (0, 4), (1, 4), (1, 5), (2, 5))
    other = swap_core(gram_part(pairs, other_at, arrays, half))
    chip_sum = ((gram_part(pairs, own_at, arrays, half) + other) * unit).astype(f16)
    chip_sum, spread = together(chip_sum, spread)
    mine = reduce_plane(chip_sum)
    chosen_piece = lax.all_to_all(spread, "col", 0, 0, tiled=True)
    c1, c2, c3, c4, c5 = (i * width_c for i in range(1, 6))
    c8 = 8 * width_c
    below, above, below3, above4 = together(
        from_col(mine[:, c1:c3], -1),
        from_col(mine[:, c2:c4], 1),
        from_col(mine[:, c3:c4], -2),
        from_col(mine[:, c4:c5], 2),
    )
    half_gram = gather_plane(jnp.concatenate([mine[:, :c2], above, above4, below, below3], axis=1))

    def along(array, axis):
        return [lax.dynamic_index_in_dim(array, lax.rem(place + k + cols, cols), axis, keepdims=False) for k in ORDER]

    def parts(blocks):
        terms = [split(block, 2) for block in blocks]
        return [t[0] for t in terms] + [t[1] for t in terms]

    blocks = parts([b[:rows] * (b[rows : rows + 1] - 1.0) for b in along(payload, 0)])
    half_gram, *blocks = together(half_gram, *blocks)
    grams = split(half_gram, 2) + split(swap_core(half_gram), 2)

    chosen_half, _ = together(chosen_piece, payload)
    chosen_half = lax.all_gather(chosen_half, CHIPS, axis=0)

    core_at = core.astype(jnp.int32).reshape(1)
    bound = (width * (1.0 + DAMPING) + 1.0) / TOP
    image_shape = jax.ShapeDtypeStruct((rows, width_c), f32)
    lane_shape = jax.ShapeDtypeStruct((rows, 128), f32)
    moment_shape = jax.ShapeDtypeStruct((8, 128), f32)
    whole_shape = jax.ShapeDtypeStruct((rows, width), f32)

    def product(first, last, blocks, scale, earlier=()):
        whole = pl.BlockSpec(memory_space=pltpu.VMEM)
        outs = ([moment_shape] if last else [image_shape, lane_shape]) + ([] if first else [whole_shape])
        return pl.pallas_call(
            functools.partial(product_kernel, first, last, bound),
            in_specs=[pl.BlockSpec(memory_space=pltpu.SMEM)]
            + [whole] * (len(blocks) + 2 + len(earlier))
            + [pl.BlockSpec(memory_space=pl.ANY)] * 4,
            out_specs=[whole] * len(outs),
            out_shape=outs,
            scratch_shapes=[pltpu.VMEM((half, c8), bf16)] * 4 + [pltpu.SemaphoreType.DMA((8, 4))],
            compiler_params=pltpu.CompilerParams(vmem_limit_bytes=20 * 2**20),
            cost_estimate=pl.CostEstimate(
                flops=6 * rows * width * width_c, bytes_accessed=10 * 2**20, transcendentals=0
            ),
        )(core_at, *blocks, expanded, scale, *earlier, *grams)

    image, scale = product(True, False, blocks, jnp.ones((rows, 128), f32))
    basis = []
    for step in range(ITERS):
        (sent,) = together(image.astype(f16))
        got, last = ring_gather(sent)
        blocks = parts([last if k == 4 else got[k] for k in ORDER])
        if step + 2 == ITERS:
            chosen_half, blocks[0] = together(chosen_half, blocks[0])
            chosen_other = swap_core(chosen_half)
        if step + 1 < ITERS:
            image, scale, scaled = product(False, False, blocks, scale)
        else:
            vector, scaled = product(False, True, blocks, scale, [b[:, :width_c] for b in basis])
        basis.append(scaled)

    picked = [chosen_half, chosen_other]
    vector, *picked = together(vector, *picked)
    vector = vector + swap_core(vector)

    vector = jnp.sum(exchange(vector, "col").reshape(cols, 8, 128), axis=0)
    info = jnp.stack([lax.rem(place + k + cols, cols) for k in ORDER] + [core]).astype(jnp.int32)
    size = 2 * picked[0].shape[0] * picked[0].shape[2]
    flat = lambda n, info: (0, 0)
    operands = [payload] * SUB + basis + picked * SUB
    return tuple(
        pl.pallas_call(
            finish_kernel,
            grid_spec=pltpu.PrefetchScalarGridSpec(
                num_scalar_prefetch=1,
                grid=(cols // SUB,),
                in_specs=[pl.BlockSpec((128, 128), flat)]
                + [
                    pl.BlockSpec((1, rows + 8, width_c), lambda n, info, u=u: (info[SUB * n + u], 0, 0))
                    for u in range(SUB)
                ]
                + [pl.BlockSpec((rows, SUB * width_c), lambda n, info: (0, n))] * ITERS
                + [
                    pl.BlockSpec(
                        (picked[0].shape[0], 1, picked[0].shape[2], width_c),
                        lambda n, info, u=u: (0, info[SUB * n + u], 0, 0),
                    )
                    for u in range(SUB)
                    for _ in range(2)
                ],
                out_specs=[pl.BlockSpec((rows, width_c), flat), pl.BlockSpec((size, rows), flat)],
                scratch_shapes=[pltpu.VMEM((8, 128), f32), pltpu.VMEM((size, rows), f32)],
            ),
            out_shape=[jax.ShapeDtypeStruct((rows, width_c), bf16), jax.ShapeDtypeStruct((size, rows), bf16)],
            compiler_params=pltpu.CompilerParams(vmem_limit_bytes=12 * 2**20),
        )(info, exchange(vector, CHIPS), *(pltpu.with_memory_space_constraint(a, pltpu.HBM) for a in operands))
    )


def solution(mesh):
    devices = mesh.devices.reshape(4, 2, 2, 8, 2)
    mesh = Mesh(devices, ("x", "yh", "core", "col", "yl"))
    placed = (P(PLANE, "col"), P(PLANE, "col"), P(PLANE, "col"), P(PLANE))
    return jax.shard_map(
        per_device,
        mesh=mesh,
        in_specs=placed,
        out_specs=(P(PLANE, "col"), P("col", PLANE)),
        check_vma=False,
    )
```

```python
import functools

import jax
import jax.numpy as jnp
from jax import lax
from jax.experimental import pallas as pl
from jax.experimental.pallas import tpu as pltpu
from jax.sharding import Mesh, PartitionSpec as P

TILE = 128
ITERS = 3
SUB = 2
DAMPING = 0.1

CHIPS = ("x", "yh", "yl")
PLANE = ("x", "yh", "core", "yl")
GRAM_UNIT = 8.0
TOP = 32768.0
bf16, f16, f32 = jnp.bfloat16, jnp.float16, jnp.float32


def from_col(array, offset):
    size = lax.axis_size("col")
    return lax.ppermute(array, "col", [(i, (i - offset) % size) for i in range(size)])


def swap_core(array):
    return lax.ppermute(array, "core", [(0, 1), (1, 0)])


def dot(left, right, side=0):
    return lax.dot_general(left, right, (((1,), (side,)), ((), ())), preferred_element_type=f32)


def together(*arrays):
    return lax.optimization_barrier(arrays)


def split(array, parts):
    terms, rest = [], array.astype(f32)
    for _ in range(parts):
        term = lax.reduce_precision(rest, 8, 7)
        terms.append(term.astype(bf16))
        rest = rest - term
    return terms


def reduce_plane(chip_sum, top):
    chips = lax.axis_size(CHIPS)
    rows, width = chip_sum.shape
    power = jnp.ceil(jnp.log2(jnp.maximum(top, 1e-30)))
    sent = (chip_sum * jnp.exp2(14.0 - power[:1, :1])).astype(f16)
    sent = jnp.concatenate([sent, jnp.broadcast_to(power[:1], (rows, 128)).astype(f16)], axis=1)

    def add(sent):
        pieces = lax.all_to_all(sent, CHIPS, 0, 0, tiled=True)
        pieces = pieces.reshape(chips, rows // chips, width + 128).astype(f32)
        return jnp.sum(pieces[:, :, :width] * jnp.exp2(pieces[:, :1, width : width + 1] - 14.0), axis=0)

    return sent, add


def gather_plane(piece):
    chips = lax.axis_size(CHIPS)
    copies = jnp.broadcast_to(piece[None], (chips,) + piece.shape).reshape(-1, piece.shape[1])
    return lax.all_to_all(copies, CHIPS, 0, 0, tiled=True)


def ring_gather(block):
    got = {0: block}
    for step in (1, 2, 3):
        got[-step], got[step] = from_col(got[1 - step], -1), from_col(got[step - 1], 1)
    half = block.shape[0] // 2
    last = jnp.concatenate([from_col(got[-3][:half], -1), from_col(got[3][half:], 1)], axis=0)
    return got, last


ORDER = (0, 1, 2, 3, 4, -1, -2, -3)


def gram_kernel(pairs, row_ref, *refs):
    arrays, out_ref, top_ref = refs[:-2], refs[-2], refs[-1]
    top = jnp.zeros((1, 1), f32)
    rows, width = out_ref.shape[0], arrays[-1].shape[1]
    for i, (left, right) in enumerate(pairs):
        start = pl.multiple_of(row_ref[0], rows)
        product = jnp.dot(arrays[left][pl.ds(start, rows), :], arrays[right][...], preferred_element_type=f32)
        out_ref[:, i * width : (i + 1) * width] = product
        top = jnp.maximum(top, jnp.max(jnp.max(jnp.abs(product), axis=0, keepdims=True), axis=1, keepdims=True))
    top_ref[...] = jnp.broadcast_to(top, top_ref.shape)


def gram_part(pairs, start, arrays, rows):
    width = arrays[-1].shape[1]
    return pl.pallas_call(
        functools.partial(gram_kernel, pairs),
        in_specs=[pl.BlockSpec(memory_space=pltpu.SMEM)] + [pl.BlockSpec(memory_space=pltpu.VMEM)] * len(arrays),
        out_specs=[pl.BlockSpec(memory_space=pltpu.VMEM)] * 2,
        out_shape=[
            jax.ShapeDtypeStruct((rows, width * len(pairs)), f32),
            jax.ShapeDtypeStruct((8, 128), f32),
        ],
        compiler_params=pltpu.CompilerParams(vmem_limit_bytes=12 * 2**20),
        cost_estimate=pl.CostEstimate(
            flops=2 * rows * width * len(pairs) * arrays[0].shape[1], bytes_accessed=8 * 2**20, transcendentals=0
        ),
    )(start, *arrays)


def product_kernel(first, last, bound, core_ref, *refs):
    refs = list(refs)

    def take(count):
        taken = refs[:count]
        del refs[:count]
        return taken

    highs, lows = take(8), take(8)
    (mask_ref,), (scale_ref,) = take(1), take(1)
    earlier = take(ITERS - 1) if last else []
    grams = take(4)
    outs = take(1 if last else 2)
    scaled_ref = None if first else take(1)[0]
    held, sems = take(4), take(1)[0]
    rows, width = highs[0].shape
    half = width // 2
    copies = []
    for n in range(8):
        group = []
        for j in range(4):
            span = pl.ds(n * width, width)
            copy = pltpu.make_async_copy(grams[j].at[:, span], held[j].at[:, span], sems.at[n, j])
            copy.start()
            group.append(copy)
        copies.append(group)
    core = core_ref[0]
    at = (pl.multiple_of(core * half, half), pl.multiple_of((1 - core) * half, half))
    sides = [jnp.zeros((rows, half), f32)] * 2
    total = jnp.zeros((rows, width), f32)
    square = jnp.zeros((rows, 1), f32)
    for n in range(8):
        high, low = highs[n][...], lows[n][...]
        value = high.astype(f32) + low.astype(f32)
        square = square + jnp.sum(value * value, axis=1, keepdims=True)
        if n == 0:
            own = value
        if not first:
            scaled_ref[:, n * width : (n + 1) * width] = value * scale_ref[:, :1]
        for copy in copies[n]:
            copy.wait()
        span = slice(n * width, (n + 1) * width)
        for side in range(2):
            gram_hi, gram_lo = held[2 * side][:, span], held[2 * side + 1][:, span]
            if n < 5:
                dims = (((1,), (1,)), ((), ()))
                x_hi, x_lo = high, low
            else:
                dims = (((1,), (0,)), ((), ()))
                x_hi, x_lo = highs[n][:, pl.ds(at[side], half)], lows[n][:, pl.ds(at[side], half)]
            both = jnp.concatenate([x_hi, x_lo], axis=0)
            part = lax.dot_general(both, gram_hi, dims, preferred_element_type=f32)
            part = part[:rows] + part[rows:]
            part += lax.dot_general(x_hi, gram_lo, dims, preferred_element_type=f32)
            if n < 5:
                sides[side] = sides[side] + part
            else:
                total = total + part
    lower = core == 0
    total += jnp.concatenate(
        [jnp.where(lower, sides[0], sides[1]), jnp.where(lower, sides[1], sides[0])], axis=1
    )
    image = (total * (1.0 / GRAM_UNIT) + DAMPING * own) * mask_ref[...]
    scale = scale_ref[:, :1]
    if last:
        vectors = [r[...] for r in earlier] + [own * scale, image * scale]
        outs[0][...] = jnp.zeros((8, 128), f32)
        for j in range(2 * ITERS):
            lanes = jnp.sum(vectors[j // 2] * vectors[(j + 1) // 2], axis=0, keepdims=True)
            outs[0][j : j + 1, :] = sum(lanes[:, i : i + 128] for i in range(0, width, 128))
    else:
        new_scale = jnp.maximum(scale * jnp.sqrt(square), 1e-30) * bound
        outs[0][...] = image * (scale / new_scale)
        outs[1][...] = jnp.broadcast_to(new_scale, outs[1].shape)


def finish_kernel(info_ref, parts_ref, *refs):
    payload_refs, basis_refs = refs[:SUB], refs[SUB : SUB + ITERS]
    picked_refs = refs[SUB + ITERS : 3 * SUB + ITERS]
    weight_ref, out_ref, lengths_ref, acc_ref = refs[3 * SUB + ITERS :]
    n = pl.program_id(0)
    rows = weight_ref.shape[0]
    size = out_ref.shape[0]

    @pl.when(n == 0)
    def _():
        total = jnp.sum(parts_ref[...].reshape(-1, 8, 128), axis=0)
        m = [jnp.sum(total[j : j + 1], axis=1, keepdims=True) for j in range(2 * ITERS)]
        one, zero = jnp.ones((1, 1), f32), jnp.zeros((1, 1), f32)
        poly = [one] + [zero] * (ITERS - 1)
        weights = [zero] * ITERS
        for step in range(ITERS):
            top = sum(poly[i] * poly[j] * m[i + j] for i in range(step + 1) for j in range(step + 1))
            low = sum(poly[i] * poly[j] * m[i + j + 1] for i in range(step + 1) for j in range(step + 1))
            length = top / low
            weights = [w + length * p for w, p in zip(weights, poly)]
            poly = [poly[i] - (length * poly[i - 1] if i else zero) for i in range(ITERS)]
        for j in range(ITERS):
            lengths_ref[j : j + 1, :] = jnp.broadcast_to(weights[j], (1, 128))
        acc_ref[...] = jnp.zeros_like(acc_ref)

    width = weight_ref.shape[1]
    for u, payload_ref in enumerate(payload_refs):
        span = slice(u * width, (u + 1) * width)
        change = sum(lengths_ref[j : j + 1, :1] * basis_refs[j][:, span] for j in range(ITERS))
        rounded = (payload_ref[0, :rows, :] * payload_ref[0, rows : rows + 1, :] - change).astype(bf16)
        if u == 0:

            @pl.when(n == 0)
            def _():
                weight_ref[...] = rounded

        for j, picked_ref in enumerate(picked_refs[2 * u : 2 * u + 2]):
            acc_ref[j * size // 2 : (j + 1) * size // 2, :] += dot(
                picked_ref[...].reshape(size // 2, width), rounded, 1
            )

    @pl.when(n == pl.num_programs(0) - 1)
    def _():
        e = lax.broadcasted_iota(jnp.int32, (size, size), 0)
        p = lax.broadcasted_iota(jnp.int32, (size, size), 1)
        block, chip_hi, core, chip_lo, inner = e >> 6, (e >> 3) & 7, (e >> 2) & 1, (e >> 1) & 1, e & 1
        found = (core ^ info_ref[8]) * (size // 2) + (chip_hi * 2 + chip_lo) * 8 + block * 2 + inner
        here = (found == p).astype(f32).astype(bf16)
        out_ref[...] = dot(here, acc_ref[...].astype(bf16)).astype(bf16)


def per_device(calibration, weight, tile_mask, token_ids):
    depth, width_c = calibration.shape
    cols = lax.axis_size("col")
    width = width_c * cols
    rows = weight.shape[0]
    plane = lax.axis_size(PLANE)
    place = lax.axis_index("col")
    core = lax.axis_index("core")
    half = width_c // 2

    plus1 = from_col(calibration, 1)
    left = calibration.T
    minus1 = from_col(left, -1)

    picks = token_ids[:, None] == lax.broadcasted_iota(jnp.int32, (token_ids.shape[0], depth), 1)
    chosen = dot(picks.astype(bf16), calibration).astype(bf16)
    each = chosen.shape[0] // plane
    squares = jnp.sum(jnp.square(calibration.astype(f32)), axis=0, keepdims=True)

    def exchange(value, axes):
        count = lax.axis_size(axes)
        copies = jnp.broadcast_to(value[None], (count,) + value.shape).reshape(-1, value.shape[1])
        return lax.all_to_all(copies, axes, 0, 0, tiled=True)

    def packed(piece, sums):
        terms = jnp.concatenate(split(sums, 3), axis=0)
        terms = jnp.broadcast_to(terms[None], (piece.shape[0],) + terms.shape)
        return jnp.concatenate([piece, terms], axis=1)

    packet = packed(chosen.reshape(plane, each, width_c), squares)
    plus1, minus1, packet = together(plus1, minus1, packet)
    packet = lax.all_to_all(packet, PLANE, 0, 0, tiled=True)

    plus2, minus2 = from_col(plus1, 1), from_col(minus1, -1)
    own_at = (core * half).astype(jnp.int32).reshape(1)
    other_at = ((1 - core) * half).astype(jnp.int32).reshape(1)
    plus2, minus2, packet = together(plus2, minus2, packet)
    squares = jnp.sum(packet[:, each:].astype(f32), axis=(0, 1))[None]
    spread = packed(packet[:, :each].reshape(cols, plane // cols * each, width_c), squares)

    expanded = jnp.broadcast_to(tile_mask.astype(f32)[:, :, None], (1, tile_mask.shape[1], TILE)).reshape(1, width_c)
    payload = jnp.concatenate([weight, jnp.broadcast_to(expanded, (8, width_c))], axis=0)
    payload, _ = together(payload, plus2)
    payload = lax.all_gather(payload, "col", axis=0)

    arrays = (left, minus1, minus2, calibration, plus1, plus2)
    pairs = ((0, 3), (0, 4), (1, 4), (1, 5), (2, 5))
    other, other_top = gram_part(pairs, other_at, arrays, half)
    other, other_top = swap_core(other), swap_core(other_top)
    own, own_top = gram_part(pairs, own_at, arrays, half)
    sent, add = reduce_plane(own + other, own_top + other_top)
    sent, spread = together(sent, spread)
    gathered = []
    for k in ORDER:
        piece = lax.dynamic_index_in_dim(spread, lax.rem(place - k + cols, cols), 0, keepdims=False)
        gathered.append(from_col(piece, k) if k else piece)
    mine = add(sent)
    gathered = jnp.stack(gathered)
    unit = GRAM_UNIT * width / jnp.sum(gathered[:, plane // cols * each :].astype(f32))
    chosen_piece = gathered[:, : plane // cols * each]
    mine = (mine * unit).astype(f16)
    c1, c2, c3, c4, c5 = (i * width_c for i in range(1, 6))
    c8 = 8 * width_c
    below, above, below3, above4 = together(
        from_col(mine[:, c1:c3], -1),
        from_col(mine[:, c2:c4], 1),
        from_col(mine[:, c3:c4], -2),
        from_col(mine[:, c4:c5], 2),
    )
    half_gram = gather_plane(jnp.concatenate([mine[:, :c2], above, above4, below, below3], axis=1))

    def along(array, axis):
        return [lax.dynamic_index_in_dim(array, lax.rem(place + k + cols, cols), axis, keepdims=False) for k in ORDER]

    def parts(blocks):
        terms = [split(block, 2) for block in blocks]
        return [t[0] for t in terms] + [t[1] for t in terms]

    blocks = parts([b[:rows] * (b[rows : rows + 1] - 1.0) for b in along(payload, 0)])
    half_gram, *blocks = together(half_gram, *blocks)
    grams = split(half_gram, 2) + split(swap_core(half_gram), 2)

    chosen_half, _ = together(chosen_piece, payload)
    chosen_half = lax.all_gather(chosen_half, CHIPS, axis=0)

    core_at = core.astype(jnp.int32).reshape(1)
    bound = (width * (1.0 + DAMPING) + 1.0) / TOP
    image_shape = jax.ShapeDtypeStruct((rows, width_c), f32)
    lane_shape = jax.ShapeDtypeStruct((rows, 128), f32)
    moment_shape = jax.ShapeDtypeStruct((8, 128), f32)
    whole_shape = jax.ShapeDtypeStruct((rows, width), f32)

    def product(first, last, blocks, scale, earlier=()):
        whole = pl.BlockSpec(memory_space=pltpu.VMEM)
        outs = ([moment_shape] if last else [image_shape, lane_shape]) + ([] if first else [whole_shape])
        return pl.pallas_call(
            functools.partial(product_kernel, first, last, bound),
            in_specs=[pl.BlockSpec(memory_space=pltpu.SMEM)]
            + [whole] * (len(blocks) + 2 + len(earlier))
            + [pl.BlockSpec(memory_space=pl.ANY)] * 4,
            out_specs=[whole] * len(outs),
            out_shape=outs,
            scratch_shapes=[pltpu.VMEM((half, c8), bf16)] * 4 + [pltpu.SemaphoreType.DMA((8, 4))],
            compiler_params=pltpu.CompilerParams(vmem_limit_bytes=20 * 2**20),
            cost_estimate=pl.CostEstimate(
                flops=6 * rows * width * width_c, bytes_accessed=10 * 2**20, transcendentals=0
            ),
        )(core_at, *blocks, expanded, scale, *earlier, *grams)

    image, scale = product(True, False, blocks, jnp.ones((rows, 128), f32))
    basis = []
    for step in range(ITERS):
        (sent,) = together(image.astype(f16))
        got, last = ring_gather(sent)
        blocks = parts([last if k == 4 else got[k] for k in ORDER])
        if step + 2 == ITERS:
            chosen_half, blocks[0] = together(chosen_half, blocks[0])
            chosen_other = swap_core(chosen_half)
        if step + 1 < ITERS:
            image, scale, scaled = product(False, False, blocks, scale)
        else:
            vector, scaled = product(False, True, blocks, scale, [b[:, :width_c] for b in basis])
        basis.append(scaled)

    picked = [chosen_half, chosen_other]
    vector, *picked = together(vector, *picked)
    vector = vector + swap_core(vector)

    vector = jnp.sum(exchange(vector, "col").reshape(cols, 8, 128), axis=0)
    info = jnp.stack([lax.rem(place + k + cols, cols) for k in ORDER] + [core]).astype(jnp.int32)
    size = 2 * picked[0].shape[0] * picked[0].shape[2]
    flat = lambda n, info: (0, 0)
    operands = [payload] * SUB + basis + picked * SUB
    return tuple(
        pl.pallas_call(
            finish_kernel,
            grid_spec=pltpu.PrefetchScalarGridSpec(
                num_scalar_prefetch=1,
                grid=(cols // SUB,),
                in_specs=[pl.BlockSpec((128, 128), flat)]
                + [
                    pl.BlockSpec((1, rows + 8, width_c), lambda n, info, u=u: (info[SUB * n + u], 0, 0))
                    for u in range(SUB)
                ]
                + [pl.BlockSpec((rows, SUB * width_c), lambda n, info: (0, n))] * ITERS
                + [
                    pl.BlockSpec(
                        (picked[0].shape[0], 1, picked[0].shape[2], width_c),
                        lambda n, info, u=u: (0, SUB * n + u, 0, 0),
                    )
                    for u in range(SUB)
                    for _ in range(2)
                ],
                out_specs=[pl.BlockSpec((rows, width_c), flat), pl.BlockSpec((size, rows), flat)],
                scratch_shapes=[pltpu.VMEM((8, 128), f32), pltpu.VMEM((size, rows), f32)],
            ),
            out_shape=[jax.ShapeDtypeStruct((rows, width_c), bf16), jax.ShapeDtypeStruct((size, rows), bf16)],
            compiler_params=pltpu.CompilerParams(vmem_limit_bytes=12 * 2**20),
        )(info, exchange(vector, CHIPS), *(pltpu.with_memory_space_constraint(a, pltpu.HBM) for a in operands))
    )


def solution(mesh):
    devices = mesh.devices.reshape(4, 2, 2, 8, 2)
    mesh = Mesh(devices, ("x", "yh", "core", "col", "yl"))
    placed = (P(PLANE, "col"), P(PLANE, "col"), P(PLANE, "col"), P(PLANE))
    return jax.shard_map(
        per_device,
        mesh=mesh,
        in_specs=placed,
        out_specs=(P(PLANE, "col"), P("col", PLANE)),
        check_vma=False,
    )
```

```python
import functools

import jax
import jax.numpy as jnp
from jax import lax
from jax.experimental import pallas as pl
from jax.experimental.pallas import tpu as pltpu
from jax.sharding import Mesh, PartitionSpec as P

TILE = 128
ITERS = 3
SUB = 2
DAMPING = 0.1

CHIPS = ("x", "yh", "yl")
PLANE = ("x", "yh", "core", "yl")
GRAM_UNIT = 8.0
TOP = 32768.0
bf16, f16, f32 = jnp.bfloat16, jnp.float16, jnp.float32


def from_col(array, offset):
    size = lax.axis_size("col")
    return lax.ppermute(array, "col", [(i, (i - offset) % size) for i in range(size)])


def swap_core(array):
    return lax.ppermute(array, "core", [(0, 1), (1, 0)])


def dot(left, right, side=0):
    return lax.dot_general(left, right, (((1,), (side,)), ((), ())), preferred_element_type=f32)


def together(*arrays):
    return lax.optimization_barrier(arrays)


def split(array, parts):
    terms, rest = [], array.astype(f32)
    for _ in range(parts):
        term = lax.reduce_precision(rest, 8, 7)
        terms.append(term.astype(bf16))
        rest = rest - term
    return terms


def reduce_plane(chip_sum, top):
    chips = lax.axis_size(CHIPS)
    rows, width = chip_sum.shape
    power = jnp.ceil(jnp.log2(jnp.maximum(top, 1e-30)))
    sent = (chip_sum * jnp.exp2(14.0 - power[:1, :1])).astype(f16)
    sent = jnp.concatenate([sent, jnp.broadcast_to(power[:1], (rows, 128)).astype(f16)], axis=1)

    def add(sent):
        pieces = lax.all_to_all(sent, CHIPS, 0, 0, tiled=True)
        pieces = pieces.reshape(chips, rows // chips, width + 128).astype(f32)
        return jnp.sum(pieces[:, :, :width] * jnp.exp2(pieces[:, :1, width : width + 1] - 14.0), axis=0)

    return sent, add


def gather_plane(piece):
    chips = lax.axis_size(CHIPS)
    copies = jnp.broadcast_to(piece[None], (chips,) + piece.shape).reshape(-1, piece.shape[1])
    return lax.all_to_all(copies, CHIPS, 0, 0, tiled=True)


def ring_gather(block):
    got = {0: block}
    for step in (1, 2, 3):
        got[-step], got[step] = from_col(got[1 - step], -1), from_col(got[step - 1], 1)
    half = block.shape[0] // 2
    last = jnp.concatenate([from_col(got[-3][:half], -1), from_col(got[3][half:], 1)], axis=0)
    return got, last


ORDER = (0, 1, 2, 3, 4, -1, -2, -3)


def gram_kernel(pairs, row_ref, *refs):
    arrays, out_ref, top_ref = refs[:-2], refs[-2], refs[-1]
    top = jnp.zeros((1, 1), f32)
    rows, width = out_ref.shape[0], arrays[-1].shape[1]
    for i, (left, right) in enumerate(pairs):
        start = pl.multiple_of(row_ref[0], rows)
        product = jnp.dot(arrays[left][pl.ds(start, rows), :], arrays[right][...], preferred_element_type=f32)
        out_ref[:, i * width : (i + 1) * width] = product
        top = jnp.maximum(top, jnp.max(jnp.max(jnp.abs(product), axis=0, keepdims=True), axis=1, keepdims=True))
    top_ref[...] = jnp.broadcast_to(top, top_ref.shape)


def gram_part(pairs, start, arrays, rows):
    width = arrays[-1].shape[1]
    return pl.pallas_call(
        functools.partial(gram_kernel, pairs),
        in_specs=[pl.BlockSpec(memory_space=pltpu.SMEM)] + [pl.BlockSpec(memory_space=pltpu.VMEM)] * len(arrays),
        out_specs=[pl.BlockSpec(memory_space=pltpu.VMEM)] * 2,
        out_shape=[
            jax.ShapeDtypeStruct((rows, width * len(pairs)), f32),
            jax.ShapeDtypeStruct((8, 128), f32),
        ],
        compiler_params=pltpu.CompilerParams(vmem_limit_bytes=12 * 2**20),
        cost_estimate=pl.CostEstimate(
            flops=2 * rows * width * len(pairs) * arrays[0].shape[1], bytes_accessed=8 * 2**20, transcendentals=0
        ),
    )(start, *arrays)


def product_kernel(first, last, bound, core_ref, *refs):
    refs = list(refs)

    def take(count):
        taken = refs[:count]
        del refs[:count]
        return taken

    highs, lows = take(8), take(8)
    (mask_ref,), (scale_ref,) = take(1), take(1)
    earlier = take(ITERS - 1) if last else []
    grams = take(4)
    outs = take(1 if last else 2)
    scaled_ref = None if first else take(1)[0]
    held, sems = take(4), take(1)[0]
    scaled, scaled_sems = (None, None) if first else take(2)
    stores = []
    rows, width = highs[0].shape
    half = width // 2
    copies = []
    for n in range(8):
        group = []
        for j in range(4):
            span = pl.ds(n * width, width)
            copy = pltpu.make_async_copy(grams[j].at[:, span], held[j].at[:, span], sems.at[n, j])
            copy.start()
            group.append(copy)
        copies.append(group)
    core = core_ref[0]
    at = (pl.multiple_of(core * half, half), pl.multiple_of((1 - core) * half, half))
    sides = [jnp.zeros((rows, half), f32)] * 2
    total = jnp.zeros((rows, width), f32)
    square = jnp.zeros((rows, 1), f32)
    for n in range(8):
        high, low = highs[n][...], lows[n][...]
        value = high.astype(f32) + low.astype(f32)
        square = square + jnp.sum(value * value, axis=1, keepdims=True)
        if n == 0:
            own = value
        if not first:
            span = pl.ds(n * width, width)
            scaled[:, n * width : (n + 1) * width] = value * scale_ref[:, :1]
            store = pltpu.make_async_copy(scaled.at[:, span], scaled_ref.at[:, span], scaled_sems.at[n])
            store.start()
            stores.append(store)
        for copy in copies[n]:
            copy.wait()
        span = slice(n * width, (n + 1) * width)
        for side in range(2):
            gram_hi, gram_lo = held[2 * side][:, span], held[2 * side + 1][:, span]
            if n < 5:
                dims = (((1,), (1,)), ((), ()))
                x_hi, x_lo = high, low
            else:
                dims = (((1,), (0,)), ((), ()))
                x_hi, x_lo = highs[n][:, pl.ds(at[side], half)], lows[n][:, pl.ds(at[side], half)]
            both = jnp.concatenate([x_hi, x_lo], axis=0)
            part = lax.dot_general(both, gram_hi, dims, preferred_element_type=f32)
            part = part[:rows] + part[rows:]
            part += lax.dot_general(x_hi, gram_lo, dims, preferred_element_type=f32)
            if n < 5:
                sides[side] = sides[side] + part
            else:
                total = total + part
    lower = core == 0
    total += jnp.concatenate(
        [jnp.where(lower, sides[0], sides[1]), jnp.where(lower, sides[1], sides[0])], axis=1
    )
    image = (total * (1.0 / GRAM_UNIT) + DAMPING * own) * mask_ref[...]
    scale = scale_ref[:, :1]
    if last:
        vectors = [r[...] for r in earlier] + [own * scale, image * scale]
        outs[0][...] = jnp.zeros((8, 128), f32)
        for j in range(2 * ITERS):
            lanes = jnp.sum(vectors[j // 2] * vectors[(j + 1) // 2], axis=0, keepdims=True)
            outs[0][j : j + 1, :] = sum(lanes[:, i : i + 128] for i in range(0, width, 128))
    else:
        new_scale = jnp.maximum(scale * jnp.sqrt(square), 1e-30) * bound
        outs[0][...] = image * (scale / new_scale)
        outs[1][...] = jnp.broadcast_to(new_scale, outs[1].shape)
    for store in stores:
        store.wait()


def finish_kernel(info_ref, parts_ref, *refs):
    payload_refs, basis_refs = refs[:SUB], refs[SUB : SUB + ITERS]
    picked_refs = refs[SUB + ITERS : 3 * SUB + ITERS]
    weight_ref, out_ref, lengths_ref, acc_ref = refs[3 * SUB + ITERS :]
    n = pl.program_id(0)
    rows = weight_ref.shape[0]
    size = out_ref.shape[0]

    @pl.when(n == 0)
    def _():
        total = jnp.sum(parts_ref[...].reshape(-1, 8, 128), axis=0)
        m = [jnp.sum(total[j : j + 1], axis=1, keepdims=True) for j in range(2 * ITERS)]
        one, zero = jnp.ones((1, 1), f32), jnp.zeros((1, 1), f32)
        poly = [one] + [zero] * (ITERS - 1)
        weights = [zero] * ITERS
        for step in range(ITERS):
            top = sum(poly[i] * poly[j] * m[i + j] for i in range(step + 1) for j in range(step + 1))
            low = sum(poly[i] * poly[j] * m[i + j + 1] for i in range(step + 1) for j in range(step + 1))
            length = top / low
            weights = [w + length * p for w, p in zip(weights, poly)]
            poly = [poly[i] - (length * poly[i - 1] if i else zero) for i in range(ITERS)]
        for j in range(ITERS):
            lengths_ref[j : j + 1, :] = jnp.broadcast_to(weights[j], (1, 128))
        acc_ref[...] = jnp.zeros_like(acc_ref)

    width = weight_ref.shape[1]
    for u, payload_ref in enumerate(payload_refs):
        span = slice(u * width, (u + 1) * width)
        change = sum(lengths_ref[j : j + 1, :1] * basis_refs[j][:, span] for j in range(ITERS))
        rounded = (payload_ref[0, :rows, :] * payload_ref[0, rows : rows + 1, :] - change).astype(bf16)
        if u == 0:

            @pl.when(n == 0)
            def _():
                weight_ref[...] = rounded

        for j, picked_ref in enumerate(picked_refs[2 * u : 2 * u + 2]):
            acc_ref[j * size // 2 : (j + 1) * size // 2, :] += dot(
                picked_ref[...].reshape(size // 2, width), rounded, 1
            )

    @pl.when(n == pl.num_programs(0) - 1)
    def _():
        e = lax.broadcasted_iota(jnp.int32, (size, size), 0)
        p = lax.broadcasted_iota(jnp.int32, (size, size), 1)
        block, chip_hi, core, chip_lo, inner = e >> 6, (e >> 3) & 7, (e >> 2) & 1, (e >> 1) & 1, e & 1
        found = (core ^ info_ref[8]) * (size // 2) + (chip_hi * 2 + chip_lo) * 8 + block * 2 + inner
        here = (found == p).astype(f32).astype(bf16)
        out_ref[...] = dot(here, acc_ref[...].astype(bf16)).astype(bf16)


def per_device(calibration, weight, tile_mask, token_ids):
    depth, width_c = calibration.shape
    cols = lax.axis_size("col")
    width = width_c * cols
    rows = weight.shape[0]
    plane = lax.axis_size(PLANE)
    place = lax.axis_index("col")
    core = lax.axis_index("core")
    half = width_c // 2

    plus1 = from_col(calibration, 1)
    left = calibration.T
    minus1 = from_col(left, -1)

    picks = token_ids[:, None] == lax.broadcasted_iota(jnp.int32, (token_ids.shape[0], depth), 1)
    chosen = dot(picks.astype(bf16), calibration).astype(bf16)
    each = chosen.shape[0] // plane
    squares = jnp.sum(jnp.square(calibration.astype(f32)), axis=0, keepdims=True)

    def exchange(value, axes):
        count = lax.axis_size(axes)
        copies = jnp.broadcast_to(value[None], (count,) + value.shape).reshape(-1, value.shape[1])
        return lax.all_to_all(copies, axes, 0, 0, tiled=True)

    def packed(piece, sums):
        terms = jnp.concatenate(split(sums, 3), axis=0)
        terms = jnp.broadcast_to(terms[None], (piece.shape[0],) + terms.shape)
        return jnp.concatenate([piece, terms], axis=1)

    packet = packed(chosen.reshape(plane, each, width_c), squares)
    plus1, minus1, packet = together(plus1, minus1, packet)
    packet = lax.all_to_all(packet, PLANE, 0, 0, tiled=True)

    plus2, minus2 = from_col(plus1, 1), from_col(minus1, -1)
    own_at = (core * half).astype(jnp.int32).reshape(1)
    other_at = ((1 - core) * half).astype(jnp.int32).reshape(1)
    plus2, minus2, packet = together(plus2, minus2, packet)
    squares = jnp.sum(packet[:, each:].astype(f32), axis=(0, 1))[None]
    spread = packed(packet[:, :each].reshape(cols, plane // cols * each, width_c), squares)

    expanded = jnp.broadcast_to(tile_mask.astype(f32)[:, :, None], (1, tile_mask.shape[1], TILE)).reshape(1, width_c)
    payload = jnp.concatenate([weight, jnp.broadcast_to(expanded, (8, width_c))], axis=0)
    payload, _ = together(payload, plus2)
    payload = lax.all_gather(payload, "col", axis=0)

    arrays = (left, minus1, minus2, calibration, plus1, plus2)
    pairs = ((0, 3), (0, 4), (1, 4), (1, 5), (2, 5))
    other, other_top = gram_part(pairs, other_at, arrays, half)
    other, other_top = swap_core(other), swap_core(other_top)
    own, own_top = gram_part(pairs, own_at, arrays, half)
    sent, add = reduce_plane(own + other, own_top + other_top)
    sent, spread = together(sent, spread)
    gathered = []
    for k in ORDER:
        piece = lax.dynamic_index_in_dim(spread, lax.rem(place - k + cols, cols), 0, keepdims=False)
        gathered.append(from_col(piece, k) if k else piece)
    mine = add(sent)
    gathered = jnp.stack(gathered)
    unit = GRAM_UNIT * width / jnp.sum(gathered[:, plane // cols * each :].astype(f32))
    chosen_piece = gathered[:, : plane // cols * each]
    mine = (mine * unit).astype(f16)
    c1, c2, c3, c4, c5 = (i * width_c for i in range(1, 6))
    c8 = 8 * width_c
    below, above, below3, above4 = together(
        from_col(mine[:, c1:c3], -1),
        from_col(mine[:, c2:c4], 1),
        from_col(mine[:, c3:c4], -2),
        from_col(mine[:, c4:c5], 2),
    )
    half_gram = gather_plane(jnp.concatenate([mine[:, :c2], above, above4, below, below3], axis=1))

    def along(array, axis):
        return [lax.dynamic_index_in_dim(array, lax.rem(place + k + cols, cols), axis, keepdims=False) for k in ORDER]

    def parts(blocks):
        terms = [split(block, 2) for block in blocks]
        return [t[0] for t in terms] + [t[1] for t in terms]

    blocks = parts([b[:rows] * (b[rows : rows + 1] - 1.0) for b in along(payload, 0)])
    half_gram, *blocks = together(half_gram, *blocks)
    grams = split(half_gram, 2) + split(swap_core(half_gram), 2)
    grams = [pltpu.with_memory_space_constraint(g, pltpu.HBM) for g in grams]

    chosen_half, _ = together(chosen_piece, payload)
    chosen_half = lax.all_gather(chosen_half, CHIPS, axis=0)

    core_at = core.astype(jnp.int32).reshape(1)
    bound = (width * (1.0 + DAMPING) + 1.0) / TOP
    image_shape = jax.ShapeDtypeStruct((rows, width_c), f32)
    lane_shape = jax.ShapeDtypeStruct((rows, 128), f32)
    moment_shape = jax.ShapeDtypeStruct((8, 128), f32)
    whole_shape = pltpu.HBM((rows, width), f32)

    def product(first, last, blocks, scale, earlier=()):
        whole = pl.BlockSpec(memory_space=pltpu.VMEM)
        outs = ([moment_shape] if last else [image_shape, lane_shape]) + ([] if first else [whole_shape])
        return pl.pallas_call(
            functools.partial(product_kernel, first, last, bound),
            in_specs=[pl.BlockSpec(memory_space=pltpu.SMEM)]
            + [whole] * (len(blocks) + 2 + len(earlier))
            + [pl.BlockSpec(memory_space=pl.ANY)] * 4,
            out_specs=[whole] * len(outs) if first else [whole] * (len(outs) - 1) + [pl.BlockSpec(memory_space=pltpu.HBM)],
            out_shape=outs,
            scratch_shapes=[pltpu.VMEM((half, c8), bf16)] * 4
            + [pltpu.SemaphoreType.DMA((8, 4))]
            + ([] if first else [pltpu.VMEM((rows, width), f32), pltpu.SemaphoreType.DMA((8,))]),
            compiler_params=pltpu.CompilerParams(vmem_limit_bytes=20 * 2**20),
            cost_estimate=pl.CostEstimate(
                flops=6 * rows * width * width_c, bytes_accessed=10 * 2**20, transcendentals=0
            ),
        )(core_at, *blocks, expanded, scale, *earlier, *grams)

    image, scale = product(True, False, blocks, jnp.ones((rows, 128), f32))
    basis = []
    for step in range(ITERS):
        (sent,) = together(image.astype(f16))
        got, last = ring_gather(sent)
        blocks = parts([last if k == 4 else got[k] for k in ORDER])
        if step + 2 == ITERS:
            chosen_half, blocks[0] = together(chosen_half, blocks[0])
            chosen_other = swap_core(chosen_half)
        if step + 1 < ITERS:
            image, scale, scaled = product(False, False, blocks, scale)
        else:
            vector, scaled = product(False, True, blocks, scale, [b[:, :width_c] for b in basis])
        basis.append(scaled)

    picked = [chosen_half, chosen_other]
    vector, *picked = together(vector, *picked)

    vector = jnp.sum(exchange(vector, ("core", "col")).reshape(-1, 8, 128), axis=0)
    info = jnp.stack([lax.rem(place + k + cols, cols) for k in ORDER] + [core]).astype(jnp.int32)
    size = 2 * picked[0].shape[0] * picked[0].shape[2]
    flat = lambda n, info: (0, 0)
    operands = [payload] * SUB + basis + picked * SUB
    return tuple(
        pl.pallas_call(
            finish_kernel,
            grid_spec=pltpu.PrefetchScalarGridSpec(
                num_scalar_prefetch=1,
                grid=(cols // SUB,),
                in_specs=[pl.BlockSpec((128, 128), flat)]
                + [
                    pl.BlockSpec((1, rows + 8, width_c), lambda n, info, u=u: (info[SUB * n + u], 0, 0))
                    for u in range(SUB)
                ]
                + [pl.BlockSpec((rows, SUB * width_c), lambda n, info: (0, n))] * ITERS
                + [
                    pl.BlockSpec(
                        (picked[0].shape[0], 1, picked[0].shape[2], width_c),
                        lambda n, info, u=u: (0, SUB * n + u, 0, 0),
                    )
                    for u in range(SUB)
                    for _ in range(2)
                ],
                out_specs=[pl.BlockSpec((rows, width_c), flat), pl.BlockSpec((size, rows), flat)],
                scratch_shapes=[pltpu.VMEM((8, 128), f32), pltpu.VMEM((size, rows), f32)],
            ),
            out_shape=[jax.ShapeDtypeStruct((rows, width_c), bf16), jax.ShapeDtypeStruct((size, rows), bf16)],
            compiler_params=pltpu.CompilerParams(vmem_limit_bytes=12 * 2**20),
        )(info, exchange(vector, CHIPS), *(pltpu.with_memory_space_constraint(a, pltpu.HBM) for a in operands))
    )


def solution(mesh):
    devices = mesh.devices.reshape(4, 2, 2, 8, 2)
    mesh = Mesh(devices, ("x", "yh", "core", "col", "yl"))
    placed = (P(PLANE, "col"), P(PLANE, "col"), P(PLANE, "col"), P(PLANE))
    return jax.shard_map(
        per_device,
        mesh=mesh,
        in_specs=placed,
        out_specs=(P(PLANE, "col"), P("col", PLANE)),
        check_vma=False,
    )
```

```python
import functools

import jax
import jax.numpy as jnp
from jax import lax
from jax.experimental import pallas as pl
from jax.experimental.pallas import tpu as pltpu
from jax.sharding import Mesh, PartitionSpec as P

TILE = 128
ITERS = 3
SUB = 2
DAMPING = 0.1

CHIPS = ("x", "yh", "yl")
PLANE = ("x", "yh", "core", "yl")
GRAM_UNIT = 8.0
TOP = 32768.0
bf16, f16, f32 = jnp.bfloat16, jnp.float16, jnp.float32


def from_col(array, offset):
    size = lax.axis_size("col")
    return lax.ppermute(array, "col", [(i, (i - offset) % size) for i in range(size)])


def swap_core(array):
    return lax.ppermute(array, "core", [(0, 1), (1, 0)])


def dot(left, right, side=0):
    return lax.dot_general(left, right, (((1,), (side,)), ((), ())), preferred_element_type=f32)


def together(*arrays):
    return lax.optimization_barrier(arrays)


def split(array, parts):
    terms, rest = [], array.astype(f32)
    for _ in range(parts):
        term = lax.reduce_precision(rest, 8, 7)
        terms.append(term.astype(bf16))
        rest = rest - term
    return terms


def reduce_plane(chip_sum, top):
    chips = lax.axis_size(CHIPS)
    rows, width = chip_sum.shape
    power = jnp.ceil(jnp.log2(jnp.maximum(top, 1e-30)))
    sent = (chip_sum * jnp.exp2(14.0 - power[:1, :1])).astype(f16)
    sent = jnp.concatenate([sent, jnp.broadcast_to(power[:1], (rows, 128)).astype(f16)], axis=1)

    def add(sent):
        pieces = lax.all_to_all(sent, CHIPS, 0, 0, tiled=True)
        pieces = pieces.reshape(chips, rows // chips, width + 128).astype(f32)
        return jnp.sum(pieces[:, :, :width] * jnp.exp2(pieces[:, :1, width : width + 1] - 14.0), axis=0)

    return sent, add


def gather_plane(piece):
    chips = lax.axis_size(CHIPS)
    copies = jnp.broadcast_to(piece[None], (chips,) + piece.shape).reshape(-1, piece.shape[1])
    return lax.all_to_all(copies, CHIPS, 0, 0, tiled=True)


def ring_gather(block):
    got = {0: block}
    for step in (1, 2, 3):
        got[-step], got[step] = from_col(got[1 - step], -1), from_col(got[step - 1], 1)
    half = block.shape[0] // 2
    last = jnp.concatenate([from_col(got[-3][:half], -1), from_col(got[3][half:], 1)], axis=0)
    return got, last


ORDER = (0, 1, 2, 3, 4, -1, -2, -3)


def gram_kernel(pairs, row_ref, *refs):
    arrays, out_ref, top_ref = refs[:-2], refs[-2], refs[-1]
    top = jnp.zeros((1, 1), f32)
    rows, width = out_ref.shape[0], arrays[-1].shape[1]
    for i, (left, right) in enumerate(pairs):
        start = pl.multiple_of(row_ref[0], rows)
        product = jnp.dot(arrays[left][pl.ds(start, rows), :], arrays[right][...], preferred_element_type=f32)
        out_ref[:, i * width : (i + 1) * width] = product
        top = jnp.maximum(top, jnp.max(jnp.max(jnp.abs(product), axis=0, keepdims=True), axis=1, keepdims=True))
    top_ref[...] = jnp.broadcast_to(top, top_ref.shape)


def gram_part(pairs, start, arrays, rows):
    width = arrays[-1].shape[1]
    return pl.pallas_call(
        functools.partial(gram_kernel, pairs),
        in_specs=[pl.BlockSpec(memory_space=pltpu.SMEM)] + [pl.BlockSpec(memory_space=pltpu.VMEM)] * len(arrays),
        out_specs=[pl.BlockSpec(memory_space=pltpu.VMEM)] * 2,
        out_shape=[
            jax.ShapeDtypeStruct((rows, width * len(pairs)), f32),
            jax.ShapeDtypeStruct((8, 128), f32),
        ],
        compiler_params=pltpu.CompilerParams(vmem_limit_bytes=12 * 2**20),
        cost_estimate=pl.CostEstimate(
            flops=2 * rows * width * len(pairs) * arrays[0].shape[1], bytes_accessed=8 * 2**20, transcendentals=0
        ),
    )(start, *arrays)


def product_kernel(first, last, bound, core_ref, *refs):
    refs = list(refs)

    def take(count):
        taken = refs[:count]
        del refs[:count]
        return taken

    highs, lows = take(8), take(8)
    (mask_ref,), (scale_ref,) = take(1), take(1)
    earlier = take(ITERS - 1) if last else []
    grams = take(4)
    outs = take(1 if last else 2)
    scaled_ref = None if first else take(1)[0]
    held, sems = take(4), take(1)[0]
    scaled, scaled_sems = (None, None) if first else take(2)
    stores = []
    rows, width = highs[0].shape
    half = width // 2
    copies = []
    for n in range(8):
        group = []
        for j in range(4):
            span = pl.ds(n * width, width)
            copy = pltpu.make_async_copy(grams[j].at[:, span], held[j].at[:, span], sems.at[n, j])
            copy.start()
            group.append(copy)
        copies.append(group)
    core = core_ref[0]
    at = (pl.multiple_of(core * half, half), pl.multiple_of((1 - core) * half, half))
    sides = [jnp.zeros((rows, half), f32)] * 2
    total = jnp.zeros((rows, width), f32)
    square = jnp.zeros((rows, 1), f32)
    for n in range(8):
        high, low = highs[n][...], lows[n][...]
        value = high.astype(f32) + low.astype(f32)
        square = square + jnp.sum(value * value, axis=1, keepdims=True)
        if n == 0:
            own = value
        if not first:
            span = pl.ds(n * width, width)
            scaled[:, n * width : (n + 1) * width] = value * scale_ref[:, :1]
            store = pltpu.make_async_copy(scaled.at[:, span], scaled_ref.at[:, span], scaled_sems.at[n])
            store.start()
            stores.append(store)
        for copy in copies[n]:
            copy.wait()
        span = slice(n * width, (n + 1) * width)
        for side in range(2):
            gram_hi, gram_lo = held[2 * side][:, span], held[2 * side + 1][:, span]
            if n < 5:
                dims = (((1,), (1,)), ((), ()))
                x_hi, x_lo = high, low
            else:
                dims = (((1,), (0,)), ((), ()))
                x_hi, x_lo = highs[n][:, pl.ds(at[side], half)], lows[n][:, pl.ds(at[side], half)]
            both = jnp.concatenate([x_hi, x_lo], axis=0)
            part = lax.dot_general(both, gram_hi, dims, preferred_element_type=f32)
            part = part[:rows] + part[rows:]
            part += lax.dot_general(x_hi, gram_lo, dims, preferred_element_type=f32)
            if n < 5:
                sides[side] = sides[side] + part
            else:
                total = total + part
    lower = core == 0
    total += jnp.concatenate(
        [jnp.where(lower, sides[0], sides[1]), jnp.where(lower, sides[1], sides[0])], axis=1
    )
    image = (total * (1.0 / GRAM_UNIT) + DAMPING * own) * mask_ref[...]
    scale = scale_ref[:, :1]
    if last:
        vectors = [r[...] for r in earlier] + [own * scale, image * scale]
        outs[0][...] = jnp.zeros((8, 128), f32)
        for j in range(2 * ITERS):
            lanes = jnp.sum(vectors[j // 2] * vectors[(j + 1) // 2], axis=0, keepdims=True)
            outs[0][j : j + 1, :] = sum(lanes[:, i : i + 128] for i in range(0, width, 128))
    else:
        new_scale = jnp.maximum(scale * jnp.sqrt(square), 1e-30) * bound
        outs[0][...] = image * (scale / new_scale)
        outs[1][...] = jnp.broadcast_to(new_scale, outs[1].shape)
    for store in stores:
        store.wait()


def finish_kernel(info_ref, parts_ref, *refs):
    payload_refs, basis_refs = refs[:SUB], refs[SUB : SUB + ITERS]
    picked_refs = refs[SUB + ITERS : 3 * SUB + ITERS]
    weight_ref, out_ref, lengths_ref, acc_ref = refs[3 * SUB + ITERS :]
    n = pl.program_id(0)
    rows = weight_ref.shape[0]
    size = out_ref.shape[0]

    @pl.when(n == 0)
    def _():
        total = jnp.sum(parts_ref[...].reshape(-1, 8, 128), axis=0)
        m = [jnp.sum(total[j : j + 1], axis=1, keepdims=True) for j in range(2 * ITERS)]
        one, zero = jnp.ones((1, 1), f32), jnp.zeros((1, 1), f32)
        poly = [one] + [zero] * (ITERS - 1)
        weights = [zero] * ITERS
        for step in range(ITERS):
            top = sum(poly[i] * poly[j] * m[i + j] for i in range(step + 1) for j in range(step + 1))
            low = sum(poly[i] * poly[j] * m[i + j + 1] for i in range(step + 1) for j in range(step + 1))
            length = top / low
            weights = [w + length * p for w, p in zip(weights, poly)]
            poly = [poly[i] - (length * poly[i - 1] if i else zero) for i in range(ITERS)]
        for j in range(ITERS):
            lengths_ref[j : j + 1, :] = jnp.broadcast_to(weights[j], (1, 128))
        acc_ref[...] = jnp.zeros_like(acc_ref)

    width = weight_ref.shape[1]
    for u, payload_ref in enumerate(payload_refs):
        span = slice(u * width, (u + 1) * width)
        change = sum(lengths_ref[j : j + 1, :1] * basis_refs[j][:, span] for j in range(ITERS))
        rounded = (payload_ref[0, :rows, :] * payload_ref[0, rows : rows + 1, :] - change).astype(bf16)
        if u == 0:

            @pl.when(n == 0)
            def _():
                weight_ref[...] = rounded

        for j, picked_ref in enumerate(picked_refs[2 * u : 2 * u + 2]):
            acc_ref[j * size // 2 : (j + 1) * size // 2, :] += dot(
                picked_ref[...].reshape(size // 2, width), rounded, 1
            )

    @pl.when(n == pl.num_programs(0) - 1)
    def _():
        e = lax.broadcasted_iota(jnp.int32, (size, size), 0)
        p = lax.broadcasted_iota(jnp.int32, (size, size), 1)
        block, chip_hi, core, chip_lo, inner = e >> 6, (e >> 3) & 7, (e >> 2) & 1, (e >> 1) & 1, e & 1
        found = (core ^ info_ref[8]) * (size // 2) + (chip_hi * 2 + chip_lo) * 8 + block * 2 + inner
        here = (found == p).astype(f32).astype(bf16)
        out_ref[...] = dot(here, acc_ref[...].astype(bf16)).astype(bf16)


def per_device(calibration, weight, tile_mask, token_ids):
    depth, width_c = calibration.shape
    cols = lax.axis_size("col")
    width = width_c * cols
    rows = weight.shape[0]
    plane = lax.axis_size(PLANE)
    place = lax.axis_index("col")
    core = lax.axis_index("core")
    half = width_c // 2

    plus1 = from_col(calibration, 1)
    left = calibration.T
    minus1 = from_col(left, -1)

    picks = token_ids[:, None] == lax.broadcasted_iota(jnp.int32, (token_ids.shape[0], depth), 1)
    chosen = dot(picks.astype(bf16), calibration).astype(bf16)
    each = chosen.shape[0] // plane
    squares = jnp.sum(jnp.square(calibration.astype(f32)), axis=0, keepdims=True)

    def exchange(value, axes):
        count = lax.axis_size(axes)
        copies = jnp.broadcast_to(value[None], (count,) + value.shape).reshape(-1, value.shape[1])
        return lax.all_to_all(copies, axes, 0, 0, tiled=True)

    def packed(piece, sums):
        terms = jnp.concatenate(split(sums, 3), axis=0)
        terms = jnp.broadcast_to(terms[None], (piece.shape[0],) + terms.shape)
        return jnp.concatenate([piece, terms], axis=1)

    packet = packed(chosen.reshape(plane, each, width_c), squares)
    plus1, minus1, packet = together(plus1, minus1, packet)
    packet = lax.all_to_all(packet, PLANE, 0, 0, tiled=True)

    plus2, minus2 = from_col(plus1, 1), from_col(minus1, -1)
    own_at = (core * half).astype(jnp.int32).reshape(1)
    other_at = ((1 - core) * half).astype(jnp.int32).reshape(1)
    plus2, minus2, packet = together(plus2, minus2, packet)
    squares = jnp.sum(packet[:, each:].astype(f32), axis=(0, 1))[None]
    spread = packed(packet[:, :each].reshape(cols, plane // cols * each, width_c), squares)

    expanded = jnp.broadcast_to(tile_mask.astype(f32)[:, :, None], (1, tile_mask.shape[1], TILE)).reshape(1, width_c)
    payload = jnp.concatenate([weight, jnp.broadcast_to(expanded, (8, width_c))], axis=0)
    payload, _ = together(payload, plus2)
    payload = lax.all_gather(payload, "col", axis=0)

    arrays = (left, minus1, minus2, calibration, plus1, plus2)
    pairs = ((0, 3), (0, 4), (1, 4), (1, 5), (2, 5))
    other, other_top = gram_part(pairs, other_at, arrays, half)
    other, other_top = swap_core(other), swap_core(other_top)
    own, own_top = gram_part(pairs, own_at, arrays, half)
    sent, add = reduce_plane(own + other, own_top + other_top)
    sent, spread = together(sent, spread)
    gathered = []
    for k in ORDER:
        piece = lax.dynamic_index_in_dim(spread, lax.rem(place - k + cols, cols), 0, keepdims=False)
        gathered.append(from_col(piece, k) if k else piece)
    mine = add(sent)
    gathered = jnp.stack(gathered)
    unit = GRAM_UNIT * width / jnp.sum(gathered[:, plane // cols * each :].astype(f32))
    chosen_piece = gathered[:, : plane // cols * each]
    mine = (mine * unit).astype(f16)
    c1, c2, c3, c4, c5 = (i * width_c for i in range(1, 6))
    c8 = 8 * width_c
    below, above, below3, above4 = together(
        from_col(mine[:, c1:c3], -1),
        from_col(mine[:, c2:c4], 1),
        from_col(mine[:, c3:c4], -2),
        from_col(mine[:, c4:c5], 2),
    )
    half_gram = gather_plane(jnp.concatenate([mine[:, :c2], above, above4, below, below3], axis=1))

    def along(array, axis):
        return [lax.dynamic_index_in_dim(array, lax.rem(place + k + cols, cols), axis, keepdims=False) for k in ORDER]

    def parts(blocks):
        terms = [split(block, 2) for block in blocks]
        return [t[0] for t in terms] + [t[1] for t in terms]

    blocks = parts([b[:rows] * (b[rows : rows + 1] - 1.0) for b in along(payload, 0)])
    half_gram, *blocks = together(half_gram, *blocks)
    grams = split(half_gram, 2) + split(swap_core(half_gram), 2)

    chosen_half, _ = together(chosen_piece, payload)
    chosen_half = lax.all_gather(chosen_half, CHIPS, axis=0)

    core_at = core.astype(jnp.int32).reshape(1)
    bound = (width * (1.0 + DAMPING) + 1.0) / TOP
    image_shape = jax.ShapeDtypeStruct((rows, width_c), f32)
    lane_shape = jax.ShapeDtypeStruct((rows, 128), f32)
    moment_shape = jax.ShapeDtypeStruct((8, 128), f32)
    whole_shape = pltpu.HBM((rows, width), f32)

    def product(first, last, blocks, scale, earlier=()):
        whole = pl.BlockSpec(memory_space=pltpu.VMEM)
        outs = ([moment_shape] if last else [image_shape, lane_shape]) + ([] if first else [whole_shape])
        return pl.pallas_call(
            functools.partial(product_kernel, first, last, bound),
            in_specs=[pl.BlockSpec(memory_space=pltpu.SMEM)]
            + [whole] * (len(blocks) + 2 + len(earlier))
            + [pl.BlockSpec(memory_space=pl.ANY)] * 4,
            out_specs=[whole] * len(outs) if first else [whole] * (len(outs) - 1) + [pl.BlockSpec(memory_space=pltpu.HBM)],
            out_shape=outs,
            scratch_shapes=[pltpu.VMEM((half, c8), bf16)] * 4
            + [pltpu.SemaphoreType.DMA((8, 4))]
            + ([] if first else [pltpu.VMEM((rows, width), f32), pltpu.SemaphoreType.DMA((8,))]),
            compiler_params=pltpu.CompilerParams(vmem_limit_bytes=20 * 2**20),
            cost_estimate=pl.CostEstimate(
                flops=6 * rows * width * width_c, bytes_accessed=10 * 2**20, transcendentals=0
            ),
        )(core_at, *blocks, expanded, scale, *earlier, *grams)

    image, scale = product(True, False, blocks, jnp.ones((rows, 128), f32))
    basis = []
    for step in range(ITERS):
        (sent,) = together(image.astype(f16))
        got, last = ring_gather(sent)
        blocks = parts([last if k == 4 else got[k] for k in ORDER])
        if step + 2 == ITERS:
            chosen_half, blocks[0] = together(chosen_half, blocks[0])
            chosen_other = swap_core(chosen_half)
        if step + 1 < ITERS:
            image, scale, scaled = product(False, False, blocks, scale)
        else:
            vector, scaled = product(False, True, blocks, scale, [b[:, :width_c] for b in basis])
        basis.append(scaled)

    picked = [chosen_half, chosen_other]
    vector, *picked = together(vector, *picked)

    vector = jnp.sum(exchange(vector, ("core", "col")).reshape(-1, 8, 128), axis=0)
    info = jnp.stack([lax.rem(place + k + cols, cols) for k in ORDER] + [core]).astype(jnp.int32)
    size = 2 * picked[0].shape[0] * picked[0].shape[2]
    flat = lambda n, info: (0, 0)
    operands = [payload] * SUB + basis + picked * SUB
    return tuple(
        pl.pallas_call(
            finish_kernel,
            grid_spec=pltpu.PrefetchScalarGridSpec(
                num_scalar_prefetch=1,
                grid=(cols // SUB,),
                in_specs=[pl.BlockSpec((128, 128), flat)]
                + [
                    pl.BlockSpec((1, rows + 8, width_c), lambda n, info, u=u: (info[SUB * n + u], 0, 0))
                    for u in range(SUB)
                ]
                + [pl.BlockSpec((rows, SUB * width_c), lambda n, info: (0, n))] * ITERS
                + [
                    pl.BlockSpec(
                        (picked[0].shape[0], 1, picked[0].shape[2], width_c),
                        lambda n, info, u=u: (0, SUB * n + u, 0, 0),
                    )
                    for u in range(SUB)
                    for _ in range(2)
                ],
                out_specs=[pl.BlockSpec((rows, width_c), flat), pl.BlockSpec((size, rows), flat)],
                scratch_shapes=[pltpu.VMEM((8, 128), f32), pltpu.VMEM((size, rows), f32)],
            ),
            out_shape=[jax.ShapeDtypeStruct((rows, width_c), bf16), jax.ShapeDtypeStruct((size, rows), bf16)],
            compiler_params=pltpu.CompilerParams(vmem_limit_bytes=12 * 2**20),
        )(info, exchange(vector, CHIPS), *(pltpu.with_memory_space_constraint(a, pltpu.HBM) for a in operands))
    )


def solution(mesh):
    devices = mesh.devices.reshape(4, 2, 2, 8, 2)
    mesh = Mesh(devices, ("x", "yh", "core", "col", "yl"))
    placed = (P(PLANE, "col"), P(PLANE, "col"), P(PLANE, "col"), P(PLANE))
    return jax.shard_map(
        per_device,
        mesh=mesh,
        in_specs=placed,
        out_specs=(P(PLANE, "col"), P("col", PLANE)),
        check_vma=False,
    )
```
